512 devices in a mesh: wide: 32 (over z, x), narrow: 16 (over y, core).
Axes of the slice: x: 4, y: 8, z: 8, core: 2. Of those that a mesh axis runs over, the one named last changes fastest.
Arguments:
- embeddings: bfloat16 [262144, 1024], P(('wide', 'narrow')), may hold values from -32 to 32
- valid: int32 [262144], P(('wide', 'narrow')), may hold values from 0 to 1, as said below
Outputs:
- whitened: bfloat16 [262144, 1024], P(('wide', 'narrow'))
The draws below stay inside these ranges and needn't reach their ends.
Inputs may be any that keep to these rules, and one draw needn't show every extreme that they name: The first row of every aligned block of 16 rows has valid = 1.
All inputs are finite; a program needn't handle non-finite values.
Results may differ from the reference program's by a relative error of at most 0.001.
Values sent between devices are 32-bit elements; how exact they have to be, the bound alone decides.
A program may use at most 64 MiB of HBM per device.

```python
import math
import jax
import jax.numpy as jnp
from jax import lax

D = 1024
ITERS = 2
ROWS = 262144
N_WIDE = 32


def draw_embeddings(key, part):
    keys = jax.random.split(key, 4)
    col_scale = jnp.exp(jax.random.uniform(keys[0], (D,), jnp.float32, 0.0, math.log(10.0))) / 3.0
    col_mean = 1.5 * jax.random.normal(keys[1], (D,), jnp.float32)
    drift = jax.random.normal(keys[2], (D,), jnp.float32)
    position = (jnp.arange(ROWS, dtype=jnp.float32) / ROWS)[:, None]
    noise = jax.random.normal(keys[3], (ROWS, D), jnp.float32)
    values = noise * col_scale + col_mean + 1.5 * position * drift
    return jnp.clip(values, -32.0, 32.0).astype(jnp.bfloat16)


def draw_valid(key, part):
    index = jnp.arange(ROWS, dtype=jnp.int32)
    ticket = jax.random.randint(jax.random.fold_in(key, 7), (ROWS,), 0, 1000, jnp.int32)
    threshold = 250 + 650 * index // ROWS
    chosen = jnp.logical_or(ticket < threshold, index % 16 == 0)
    return chosen.astype(jnp.int32)


def setup_inputs(seed: int = 0) -> dict:
    streams_of = jax.random.split(jax.random.key(seed), 3)
    embeddings = draw_embeddings(jax.random.fold_in(streams_of[2], 71), 0)
    valid = draw_valid(jax.random.fold_in(streams_of[2], 71), 0)
    return dict(embeddings=embeddings, valid=valid)


def reference(embeddings, valid):
    mask_half = valid.astype(jnp.bfloat16)
    count = jnp.sum(valid.astype(jnp.float32))
    blocks_x = embeddings.reshape(N_WIDE, -1, D)
    blocks_m = mask_half.reshape(N_WIDE, -1)

    def accumulate(state, item):
        gram, sums = state
        block_x, block_m = item
        masked = block_x * block_m[:, None]
        gram = gram + lax.dot_general(masked, block_x, (((0,), (0,)), ((), ())), preferred_element_type=jnp.float32)
        sums = sums + jnp.dot(block_m[None, :], block_x, preferred_element_type=jnp.float32)[0]
        return ((gram, sums), None)
    start_state = (jnp.zeros((D, D), jnp.float32), jnp.zeros((D,), jnp.float32))
    (gram, sums), _ = lax.scan(accumulate, start_state, (blocks_x, blocks_m))
    center = sums / count
    scatter = gram - sums[:, None] * center[None, :] - center[:, None] * sums[None, :] + count * center[:, None] * center[None, :]
    cov = scatter / count
    trace_cov = jnp.trace(cov)
    square_sum = jnp.sum(cov * cov)
    ridge_add = 0.05 * trace_cov / D + 1e-06
    norm_frob = jnp.sqrt(square_sum + 2.0 * ridge_add * trace_cov + D * ridge_add * ridge_add)
    identity = jnp.eye(D, dtype=jnp.float32)
    base = (cov + ridge_add * identity) / norm_frob
    root = (3.0 * identity - base) / 2.0
    for _ in range(ITERS - 1):
        first = jnp.dot(base, root, precision=lax.Precision.HIGHEST, preferred_element_type=jnp.float32)
        second = jnp.dot(first, root, precision=lax.Precision.HIGHEST, preferred_element_type=jnp.float32)
        factor = (3.0 * identity - second) / 2.0
        root = jnp.dot(factor, root, precision=lax.Precision.HIGHEST, preferred_element_type=jnp.float32)

    def whiten_block(block_x):
        shifted = block_x.astype(jnp.float32) - center
        product = jnp.dot(shifted, root, precision=lax.Precision.HIGHEST, preferred_element_type=jnp.float32)
        return (product / jnp.sqrt(norm_frob)).astype(jnp.bfloat16)
    return lax.map(whiten_block, blocks_x).reshape(ROWS, D)
```

```python
import functools

import jax
import jax.numpy as jnp
from jax import lax
from jax.experimental import pallas as pl
from jax.experimental.pallas import tpu as pltpu
from jax.sharding import PartitionSpec as P

MESH = pl.DeviceIdType.MESH
F32 = jnp.float32
BF16 = jnp.bfloat16

SIZE = {"z": 8, "x": 4, "y": 8, "c": 2}
BLK = 128
NB = 8
HALF_ROWS = ((0, 3, 4, 7), (1, 2, 5, 6))
A1X, A2X = 256, 192
AX = A1X + A2X
A1P, A2P = A1X // 8, A2X // 8
B0 = 4 * AX
C0 = B0 + 256
D0 = C0 + 256
HALF = D0 + 8
FAR_8 = (4, 3, 5, 2, 6, 1, 7)
FAR_4 = (2, 1, 3)


def block_place(i, j):
    half = 0 if i in HALF_ROWS[0] else 1
    row = 0
    for k in HALF_ROWS[half]:
        if k == i:
            break
        row += NB - k
    return half, (row + j - i) * BLK


def coords():
    w, n = lax.axis_index("wide"), lax.axis_index("narrow")
    return {"z": w // 4, "x": w % 4, "y": n // 2, "c": n % 2}


def moved(me, axis, step):
    at = dict(me)
    at[axis] = lax.rem(me[axis] + step + SIZE[axis], SIZE[axis])
    return at


def ident(at):
    return (at["z"] * 4 + at["x"], at["y"] * 2 + at["c"])


def order(axis):
    return {"x": FAR_4, "y": FAR_8, "z": FAR_8, "c": (1,)}[axis]


def rows(start, size):
    return pl.ds(pl.multiple_of(start, 8), size)


def pool_kernel(
    x_ref, valid_ref, out_ref,
    g, got, acc,
    r1a, r1b, r1c, r1d, s1a, s1b, s1c, s1d,
    r2a, r2e, r2b, r2c, r2d, s2a, s2e, s2b, s2c, s2d,
    r3a, r3e, r3b, r3c, r3d,
    send_sem, recv_sem,
):
    me = coords()
    core = me["c"]
    barrier = pltpu.get_barrier_semaphore()
    count = 0
    for axis in ("z", "y", "x", "c"):
        for step in order(axis):
            pl.semaphore_signal(
                barrier, inc=1, device_id=ident(moved(me, axis, step)), device_id_type=MESH
            )
            count += 1

    mask = valid_ref[...].astype(F32)
    mask_half = mask.astype(BF16)
    for half in range(2):
        for i in HALF_ROWS[half]:
            left = x_ref[:, i * BLK:(i + 1) * BLK].T * mask_half
            panel = jnp.dot(left, x_ref[:, i * BLK:], preferred_element_type=F32)
            for j in range(i, NB):
                _, row = block_place(i, j)
                g[half, row:row + BLK, :] = panel[:, (j - i) * BLK:(j - i + 1) * BLK]
    sums = jnp.dot(
        jnp.broadcast_to(mask_half, (16, mask.shape[1])), x_ref[...], preferred_element_type=F32
    )
    for i in range(NB):
        g[0, D0 + i:D0 + i + 1, :] = sums[0:1, i * BLK:(i + 1) * BLK]
    g[1, D0:D0 + 8, :] = jnp.broadcast_to(jnp.sum(mask, axis=1, keepdims=True), (8, BLK))

    pl.semaphore_wait(barrier, count)

    used = []

    def copy(src, dst, axis, step):
        at = len(used)
        made = pltpu.make_async_remote_copy(
            src_ref=src, dst_ref=dst, send_sem=send_sem.at[at], recv_sem=recv_sem.at[at],
            device_id=ident(moved(me, axis, step)), device_id_type=MESH,
        )
        used.append(made)
        made.start()
        return made

    def arrive(copies):
        for made in copies:
            made.wait_recv()

    cuts = [(B0, HALF - B0)] + [(j * AX, AX) for j in range(4)]
    pair = [
        copy(g.at[1 - core, pl.ds(start, size)], got.at[pl.ds(start, size)], "c", 1)
        for start, size in cuts
    ]
    pair[0].wait_recv()
    acc[B0:HALF, :] = g[core, B0:HALF, :] + got[B0:HALF, :]
    w1b = [copy(acc.at[rows(B0 + 32 * moved(me, "y", s)["y"], 32)], r1b.at[s - 1], "y", s) for s in FAR_8]
    w1c = [copy(acc.at[rows(C0 + 32 * moved(me, "z", s)["z"], 32)], r1c.at[s - 1], "z", s) for s in FAR_8]
    w1d = [copy(acc.at[pl.ds(D0, 8)], r1d.at[s - 1], "x", s) for s in FAR_4]
    arrive(pair[1:])
    acc[0:B0, :] = g[core, 0:B0, :] + got[0:B0, :]
    w1a = [copy(acc.at[rows(AX * moved(me, "x", s)["x"], AX)], r1a.at[s - 1], "x", s) for s in FAR_4]

    def total(own, parts, n):
        value = own
        for k in range(n):
            value = value + parts[k]
        return value

    arrive(w1d)
    s1d[...] = total(acc[D0:HALF, :], r1d, 3)
    w2d = [copy(s1d, r2d.at[s - 1], "y", s) for s in FAR_8]
    arrive(w1a)
    s1a[...] = total(acc[rows(AX * me["x"], AX), :], r1a, 3)
    w2a = [copy(s1a.at[rows(A1P * moved(me, "y", s)["y"], A1P)], r2a.at[s - 1], "y", s) for s in FAR_8]
    w2e = [copy(s1a.at[rows(A1X + A2P * moved(me, "z", s)["z"], A2P)], r2e.at[s - 1], "z", s) for s in FAR_8]
    arrive(w1b)
    s1b[...] = total(acc[rows(B0 + 32 * me["y"], 32), :], r1b, 7)
    w2b = [copy(s1b.at[rows(8 * moved(me, "x", s)["x"], 8)], r2b.at[s - 1], "x", s) for s in FAR_4]
    arrive(w1c)
    s1c[...] = total(acc[rows(C0 + 32 * me["z"], 32), :], r1c, 7)
    w2c = [copy(s1c.at[rows(8 * moved(me, "x", s)["x"], 8)], r2c.at[s - 1], "x", s) for s in FAR_4]

    arrive(w2d)
    s2d[...] = total(s1d[...], r2d, 7)
    w3d = [copy(s2d, r3d.at[s - 1], "z", s) for s in FAR_8]
    arrive(w2a)
    s2a[...] = total(s1a[rows(A1P * me["y"], A1P), :], r2a, 7)
    w3a = [copy(s2a, r3a.at[s - 1], "z", s) for s in FAR_8]
    arrive(w2e)
    s2e[...] = total(s1a[rows(A1X + A2P * me["z"], A2P), :], r2e, 7)
    w3e = [copy(s2e, r3e.at[s - 1], "y", s) for s in FAR_8]
    arrive(w2b)
    s2b[...] = total(s1b[rows(8 * me["x"], 8), :], r2b, 3)
    w3b = [copy(s2b, r3b.at[s - 1], "z", s) for s in FAR_8]
    arrive(w2c)
    s2c[...] = total(s1c[rows(8 * me["x"], 8), :], r2c, 3)
    w3c = [copy(s2c, r3c.at[s - 1], "y", s) for s in FAR_8]

    def share(start, size, axis):
        piece = out_ref.at[core, rows(start, size)]
        return [copy(piece, piece, axis, s) for s in order(axis)]

    ax = AX * me["x"]
    a_at, e_at = ax + A1P * me["y"], ax + A1X + A2P * me["z"]
    b_at, c_at = B0 + 32 * me["y"] + 8 * me["x"], C0 + 32 * me["z"] + 8 * me["x"]
    arrive(w3d)
    out_ref[core, D0:HALF, :] = total(s2d[...], r3d, 7)
    w6 = share(D0, 8, "c")
    arrive(w3a)
    out_ref[core, rows(a_at, A1P), :] = total(s2a[...], r3a, 7)
    w4a = share(a_at, A1P, "y")
    arrive(w3e)
    out_ref[core, rows(e_at, A2P), :] = total(s2e[...], r3e, 7)
    w4e = share(e_at, A2P, "z")
    arrive(w3b)
    out_ref[core, rows(b_at, 8), :] = total(s2b[...], r3b, 7)
    w4b = share(b_at, 8, "x")
    arrive(w3c)
    out_ref[core, rows(c_at, 8), :] = total(s2c[...], r3c, 7)
    w4c = share(c_at, 8, "x")

    arrive(w4b)
    w5b = share(B0 + 32 * me["y"], 32, "y")
    arrive(w4c)
    w5c = share(C0 + 32 * me["z"], 32, "z")
    arrive(w4a)
    w5a = share(ax, A1X, "x")
    arrive(w4e)
    w5e = share(ax + A1X, A2X, "x")
    w6 += share(ax, AX, "c")
    for k, s in enumerate(FAR_4):
        w5a[k].wait_recv()
        w5e[k].wait_recv()
        w6 += share(AX * moved(me, "x", -s)["x"], AX, "c")
    arrive(w5b)
    w6 += share(B0, 256, "c")
    arrive(w5c)
    w6 += share(C0, 256, "c")
    arrive(w6)
    for made in used:
        made.wait_send()


N_COPIES = 5 + 7 + 7 + 3 + 3 + 7 * 3 + 3 * 2 + 7 * 5 + 7 * 2 + 3 * 2 + 7 * 2 + 3 * 2 + 7


def pool(x, valid):
    part = lambda n, r: pltpu.VMEM((n, r, BLK), F32)
    flat = lambda r: pltpu.VMEM((r, BLK), F32)
    whole = pl.BlockSpec(memory_space=pltpu.VMEM)
    return pl.pallas_call(
        pool_kernel,
        name="pool",
        out_shape=jax.ShapeDtypeStruct((2, HALF, BLK), F32),
        in_specs=[whole, whole],
        out_specs=whole,
        scratch_shapes=[
            part(2, HALF), flat(HALF), flat(HALF),
            part(3, AX), part(7, 32), part(7, 32), part(3, 8), flat(AX), flat(32), flat(32), flat(8),
            part(7, A1P), part(7, A2P), part(3, 8), part(3, 8), part(7, 8),
            flat(A1P), flat(A2P), flat(8), flat(8), flat(8),
            part(7, A1P), part(7, A2P), part(7, 8), part(7, 8), part(7, 8),
            pltpu.SemaphoreType.DMA((N_COPIES,)), pltpu.SemaphoreType.DMA((N_COPIES,)),
        ],
        compiler_params=pltpu.CompilerParams(
            collective_id=0, has_side_effects=True, vmem_limit_bytes=40 * 2**20
        ),
    )(x, valid)


def split(value):
    high = value.astype(BF16)
    return high, (value - high.astype(F32)).astype(BF16)


def white_kernel(f_ref, x_ref, o_ref, b, b2, bh, bl, ph, pp, qh, ql):
    width = NB * BLK
    count = f_ref[1, D0:D0 + 1, :]
    inverse = 1.0 / count
    sums = f_ref[0, D0:D0 + 8, :]
    center = sums / count
    diag = (
        lax.broadcasted_iota(jnp.int32, (BLK, BLK), 0)
        == lax.broadcasted_iota(jnp.int32, (BLK, BLK), 1)
    )
    eye = diag.astype(F32)

    def at(i):
        return slice(i * BLK, (i + 1) * BLK)

    trace = jnp.zeros((BLK, BLK), F32)
    square = jnp.zeros((BLK, BLK), F32)
    for i in range(NB):
        column = jnp.broadcast_to(sums[i:i + 1, :], (BLK, BLK)).T
        for j in range(i, NB):
            half, row = block_place(i, j)
            scatter = f_ref[half, row:row + BLK, :] - column * center[j:j + 1, :]
            cov = scatter * inverse
            if i == j:
                trace = trace + jnp.where(diag, cov, 0.0)
                square = square + cov * cov
            else:
                square = square + 2.0 * (cov * cov)
            b[at(i), at(j)] = cov
    trace = jnp.sum(trace, axis=(0, 1), keepdims=True)
    square = jnp.sum(square, axis=(0, 1), keepdims=True)
    ridge = 0.05 * trace / width + 1e-06
    norm = jnp.sqrt(square + 2.0 * ridge * trace + width * ridge * ridge)
    inv_norm = 1.0 / norm

    def put(value, i, j, high, low):
        h, l = split(value)
        high[at(i), at(j)] = h
        low[at(i), at(j)] = l
        if i != j:
            h, l = split(value.T)
            high[at(j), at(i)] = h
            low[at(j), at(i)] = l

    for i in range(NB):
        for j in range(i, NB):
            value = b[at(i), at(j)]
            if i == j:
                value = value + ridge * eye
            value = value * inv_norm
            b[at(i), at(j)] = value
            put(value, i, j, bh, bl)

    step = 2 * BLK

    def product(p, lh, ll, rh, rl):
        take, rest = slice(p * step, (p + 1) * step), slice(p * step, width)
        return (
            jnp.dot(lh[take, :], rh[:, rest], preferred_element_type=F32)
            + jnp.dot(lh[take, :], rl[:, rest], preferred_element_type=F32)
            + jnp.dot(ll[take, :], rh[:, rest], preferred_element_type=F32)
        )

    for p in range(NB // 2):
        b2[p * step:(p + 1) * step, p * step:] = product(p, bh, bl, bh, bl)
    for i in range(NB):
        for j in range(i, NB):
            value = b2[at(i), at(j)]
            put(value, i, j, ph, pp)
            put(value - 9.0 * b[at(i), at(j)], i, j, qh, ql)
    scale = lax.rsqrt(norm) / 16.0
    for p in range(NB // 2):
        high_part = product(p, ph, pp, qh, ql)
        for i in (2 * p, 2 * p + 1):
            for j in range(i, NB):
                value = high_part[(i - 2 * p) * BLK:(i - 2 * p + 1) * BLK, (j - 2 * p) * BLK:(j - 2 * p + 1) * BLK]
                value = value + (27.0 * b2[at(i), at(j)] - 39.0 * b[at(i), at(j)])
                if i == j:
                    value = value + 36.0 * eye
                put(value * scale, i, j, bh, bl)

    line = jnp.concatenate([center[i:i + 1, :] for i in range(NB)], axis=1)
    c_high, c_rest = split(line)
    c_rest = line - c_high.astype(F32)
    c_mid = c_rest.astype(BF16).astype(F32)
    c_low = c_rest - c_mid
    which = lax.broadcasted_iota(jnp.int32, (16, width), 0)
    parts = jnp.where(
        which == 0, c_high.astype(F32),
        jnp.where(which == 1, c_mid, jnp.where(which == 2, c_low, 0.0)),
    ).astype(BF16)
    shift = jnp.dot(parts, bh[...], preferred_element_type=F32) + jnp.dot(
        parts, bl[...], preferred_element_type=F32
    )
    shift = jnp.sum(shift, axis=0, keepdims=True)
    for r in range(0, x_ref.shape[0], step):
        for c in range(0, width, 2 * step):
            value = jnp.dot(x_ref[r:r + step, :], bh[:, c:c + 2 * step], preferred_element_type=F32)
            value += jnp.dot(x_ref[r:r + step, :], bl[:, c:c + 2 * step], preferred_element_type=F32)
            o_ref[r:r + step, c:c + 2 * step] = (value - shift[:, c:c + 2 * step]).astype(BF16)


def white(pooled, x):
    width = NB * BLK
    whole = pl.BlockSpec(memory_space=pltpu.VMEM)
    return pl.pallas_call(
        white_kernel,
        name="white",
        out_shape=jax.ShapeDtypeStruct(x.shape, BF16),
        in_specs=[whole, whole],
        out_specs=whole,
        scratch_shapes=[pltpu.VMEM((width, width), F32)] * 2 + [pltpu.VMEM((width, width), BF16)] * 6,
        compiler_params=pltpu.CompilerParams(vmem_limit_bytes=48 * 2**20),
    )(pooled, x)


def on_device(embeddings, valid):
    return white(pool(embeddings, valid[None, :]), embeddings)


def solution(mesh):
    in_specs = (P(("wide", "narrow"), None), P(("wide", "narrow")))
    return jax.shard_map(
        on_device, mesh=mesh, in_specs=in_specs, out_specs=P(("wide", "narrow"), None), check_vma=False
    )
```

```python
import functools

import jax
import jax.numpy as jnp
from jax import lax
from jax.experimental import pallas as pl
from jax.experimental.pallas import tpu as pltpu
from jax.sharding import PartitionSpec as P

MESH = pl.DeviceIdType.MESH
F32 = jnp.float32
BF16 = jnp.bfloat16

SIZE = {"z": 8, "x": 4, "y": 8, "c": 2}
BLK = 128
NB = 8
HALF_ROWS = ((0, 3, 4, 7), (1, 2, 5, 6))
A1X, A2X = 192, 128
AX = A1X + A2X
A1P, A2P = A1X // 8, A2X // 8
BY, BX = 64, 16
B0 = 4 * AX
C0 = B0 + 8 * BY
D0 = C0 + 8 * BY
HALF = D0 + 8
GX = AX + 8
GB = 4 * GX
GC = GB + 8 * BY
GHALF = GC + 8 * BY
N_COPIES = 120
FAR_8 = (4, 3, 5, 2, 6, 1, 7)
FAR_4 = (2, 1, 3)


def block_place(i, j):
    half = 0 if i in HALF_ROWS[0] else 1
    row = 0
    for k in HALF_ROWS[half]:
        if k == i:
            break
        row += NB - k
    return half, (row + j - i) * BLK


def coords():
    w, n = lax.axis_index("wide"), lax.axis_index("narrow")
    return {"z": w // 4, "x": w % 4, "y": n // 2, "c": n % 2}


def moved(me, axis, step):
    at = dict(me)
    at[axis] = lax.rem(me[axis] + step + SIZE[axis], SIZE[axis])
    return at


def ident(at):
    return (at["z"] * 4 + at["x"], at["y"] * 2 + at["c"])


def order(axis):
    return {"x": FAR_4, "y": FAR_8, "z": FAR_8, "c": (1,)}[axis]


def rows(start, size):
    return pl.ds(pl.multiple_of(start, 8), size)


def summed_row(row):
    return row // AX * GX + row % AX if row < B0 else row - B0 + GB


def total(own, parts):
    value = own
    for k in range(parts.shape[0]):
        value = value + parts[k]
    return value


def pool_kernel(
    x_hbm, valid_hbm, out_ref,
    x_ref, valid_ref, g, got, acc,
    r1x, r1y, r1z, s1a, s1e, s1x, r2x, r2y, r2z, s2z, s2y, r3z, r3y,
    load_sem, send_sem, recv_sem,
):
    me = coords()
    core = me["c"]
    barrier = pltpu.get_barrier_semaphore()
    count = 0
    for axis in ("z", "y", "x", "c"):
        for step in order(axis):
            pl.semaphore_signal(
                barrier, inc=1, device_id=ident(moved(me, axis, step)), device_id_type=MESH
            )
            count += 1
    loads = [
        pltpu.make_async_copy(x_hbm, x_ref, load_sem.at[0]),
        pltpu.make_async_copy(valid_hbm, valid_ref, load_sem.at[1]),
    ]
    for load in loads:
        load.start()
    for load in loads:
        load.wait()

    mask = valid_ref[...].astype(F32)
    mask_half = mask.astype(BF16)
    for half in range(2):
        for i in HALF_ROWS[half]:
            left = x_ref[:, i * BLK:(i + 1) * BLK].T * mask_half
            panel = jnp.dot(left, x_ref[:, i * BLK:], preferred_element_type=F32)
            for j in range(i, NB):
                _, row = block_place(i, j)
                for k in range(0, BLK, 64):
                    to = summed_row(row + k)
                    g[half, to:to + 64, :] = panel[k:k + 64, (j - i) * BLK:(j - i + 1) * BLK]
    sums = jnp.dot(
        jnp.broadcast_to(mask_half, (16, mask.shape[1])), x_ref[...], preferred_element_type=F32
    )
    valid_count = jnp.broadcast_to(jnp.sum(mask, axis=1, keepdims=True), (8, BLK))
    for part in range(4):
        to = part * GX + AX
        for i in range(NB):
            g[0, to + i:to + i + 1, :] = sums[0:1, i * BLK:(i + 1) * BLK]
        g[1, to:to + 8, :] = valid_count

    pl.semaphore_wait(barrier, count)

    used = []

    def copy(src, dst, axis, step):
        at = len(used)
        made = pltpu.make_async_remote_copy(
            src_ref=src, dst_ref=dst, send_sem=send_sem.at[at], recv_sem=recv_sem.at[at],
            device_id=ident(moved(me, axis, step)), device_id_type=MESH,
        )
        used.append(made)
        made.start()
        return made

    def arrive(copies):
        for made in copies:
            made.wait_recv()

    def beside(axis, step):
        return moved(me, axis, step)[axis]

    cuts = [pl.ds(GB, GHALF - GB)] + [rows(GX * beside("x", s), GX) for s in FAR_4 + (0,)]
    pair = [copy(g.at[1 - core, cut], got.at[cut], "c", 1) for cut in cuts]

    def add_pair(k):
        pair[k].wait_recv()
        acc[cuts[k], :] = g[core, cuts[k], :] + got[cuts[k], :]

    add_pair(0)
    w1y, w1z = [], []
    for s in FAR_8:
        w1y.append(copy(acc.at[rows(GB + BY * beside("y", s), BY)], r1y.at[s - 1], "y", s))
        w1z.append(copy(acc.at[rows(GC + BY * beside("z", s), BY)], r1z.at[s - 1], "z", s))
    w1x = []
    for k, s in enumerate(FAR_4):
        add_pair(k + 1)
        w1x.append(copy(acc.at[cuts[k + 1]], r1x.at[s - 1], "x", s))
    add_pair(4)

    arrive(w1x)
    s1a[...] = total(acc[rows(GX * me["x"], GX), :], r1x)
    w2y = [copy(s1a.at[rows(A1P * beside("y", s), A1P)], r2y.at[s - 1], "y", s) for s in FAR_8]
    for k in range(8):
        s1e[k, 0:A2P, :] = s1a[A1X + A2P * k:A1X + A2P * (k + 1), :]
        s1e[k, A2P:A2P + 8, :] = s1a[AX:GX, :]
    w2z = [copy(s1e.at[beside("z", s)], r2z.at[s - 1], "z", s) for s in FAR_8]
    arrive(w1y)
    value = total(acc[rows(GB + BY * me["y"], BY), :], r1y)
    for k in range(4):
        s1x[k, 0:BX, :] = value[BX * k:BX * (k + 1), :]
    arrive(w1z)
    value = total(acc[rows(GC + BY * me["z"], BY), :], r1z)
    for k in range(4):
        s1x[k, BX:2 * BX, :] = value[BX * k:BX * (k + 1), :]
    w2x = [copy(s1x.at[beside("x", s)], r2x.at[s - 1], "x", s) for s in FAR_4]

    arrive(w2y)
    s2z[0:A1P, :] = total(s1a[rows(A1P * me["y"], A1P), :], r2y)
    arrive(w2x)
    value = total(s1x[me["x"]], r2x)
    s2z[A1P:A1P + BX, :] = value[0:BX, :]
    w3z = [copy(s2z, r3z.at[s - 1], "z", s) for s in FAR_8]
    s2y[A2P + 8:A2P + 8 + BX, :] = value[BX:2 * BX, :]
    arrive(w2z)
    s2y[0:A2P + 8, :] = total(s1e[me["z"]], r2z)
    w3y = [copy(s2y, r3y.at[s - 1], "y", s) for s in FAR_8]

    def share(start, size, axis):
        piece = out_ref.at[core, rows(start, size)]
        return [copy(piece, piece, axis, s) for s in order(axis)]

    ax = AX * me["x"]
    a_at, e_at = ax + A1P * me["y"], ax + A1X + A2P * me["z"]
    b_at, c_at = B0 + BY * me["y"], C0 + BY * me["z"]
    arrive(w3z)
    value = total(s2z[...], r3z)
    out_ref[core, rows(b_at + BX * me["x"], BX), :] = value[A1P:A1P + BX, :]
    w4b = share(b_at + BX * me["x"], BX, "x")
    out_ref[core, rows(a_at, A1P), :] = value[0:A1P, :]
    w4a = share(a_at, A1P, "y")
    arrive(w3y)
    value = total(s2y[...], r3y)
    out_ref[core, rows(c_at + BX * me["x"], BX), :] = value[A2P + 8:A2P + 8 + BX, :]
    w4c = share(c_at + BX * me["x"], BX, "x")
    out_ref[core, rows(e_at, A2P), :] = value[0:A2P, :]
    w4e = share(e_at, A2P, "z")
    out_ref[core, D0:HALF, :] = value[A2P:A2P + 8, :]

    arrive(w4b)
    w5b = share(b_at, BY, "y")
    arrive(w4c)
    w5c = share(c_at, BY, "z")
    arrive(w4a)
    w5a = share(ax, A1X, "x")
    arrive(w4e)
    w5e = share(ax + A1X, A2X, "x")
    w6 = share(D0, 8, "c") + share(ax, AX, "c") + share(b_at, BY, "c") + share(c_at, BY, "c")
    for s in (1, 7, 2, 6, 3, 5, 4):
        k = FAR_8.index(s)
        w5b[k].wait_recv()
        w6 += share(B0 + BY * beside("y", -s), BY, "c")
        w5c[k].wait_recv()
        w6 += share(C0 + BY * beside("z", -s), BY, "c")
        if s in (7, 6, 5):
            k = (7, 6, 5).index(s)
            s = (1, 3, 2)[k]
            k = FAR_4.index(s)
            w5a[k].wait_recv()
            w5e[k].wait_recv()
            w6 += share(AX * beside("x", -s), AX, "c")
    arrive(w6)
    for made in used:
        made.wait_send()


def pool(x, valid):
    part = lambda n, r: pltpu.VMEM((n, r, BLK), F32)
    flat = lambda r: pltpu.VMEM((r, BLK), F32)
    return pl.pallas_call(
        pool_kernel,
        name="pool",
        out_shape=jax.ShapeDtypeStruct((2, HALF, BLK), F32),
        in_specs=[pl.BlockSpec(memory_space=pltpu.HBM)] * 2,
        out_specs=pl.BlockSpec(memory_space=pltpu.VMEM),
        scratch_shapes=[
            pltpu.VMEM(x.shape, BF16), pltpu.VMEM(valid.shape, jnp.int32),
            part(2, GHALF), flat(GHALF), flat(GHALF),
            part(3, GX), part(7, BY), part(7, BY),
            flat(GX), part(8, A2P + 8), part(4, 2 * BX),
            part(3, 2 * BX), part(7, A1P), part(7, A2P + 8),
            flat(A1P + BX), flat(A2P + 8 + BX), part(7, A1P + BX), part(7, A2P + 8 + BX),
            pltpu.SemaphoreType.DMA((2,)),
            pltpu.SemaphoreType.DMA((N_COPIES,)), pltpu.SemaphoreType.DMA((N_COPIES,)),
        ],
        compiler_params=pltpu.CompilerParams(
            collective_id=0, has_side_effects=True, vmem_limit_bytes=40 * 2**20
        ),
    )(x, valid)


def split(value):
    high = value.astype(BF16)
    return high, (value - high.astype(F32)).astype(BF16)


def white_kernel(f_ref, x_hbm, o_hbm, x_ref, o_ref, b, b2, bh, bl, sh, sl, load_sem, store_sem):
    width = NB * BLK
    n_rows = x_hbm.shape[0]
    load = pltpu.make_async_copy(x_hbm, x_ref.at[pl.ds(0, n_rows)], load_sem)
    load.start()
    count = f_ref[1, D0:D0 + 1, :]
    inverse = 1.0 / count
    sums = f_ref[0, D0:D0 + 8, :]
    center = sums / count
    diag = (
        lax.broadcasted_iota(jnp.int32, (BLK, BLK), 0)
        == lax.broadcasted_iota(jnp.int32, (BLK, BLK), 1)
    )
    eye = diag.astype(F32)

    def at(i):
        return slice(i * BLK, (i + 1) * BLK)

    trace = jnp.zeros((BLK, BLK), F32)
    square = jnp.zeros((BLK, BLK), F32)
    for i in range(NB):
        column = jnp.broadcast_to(sums[i:i + 1, :], (BLK, BLK)).T
        for j in range(i, NB):
            half, row = block_place(i, j)
            scatter = f_ref[half, row:row + BLK, :] - column * center[j:j + 1, :]
            cov = scatter * inverse
            if i == j:
                trace = trace + jnp.where(diag, cov, 0.0)
                square = square + cov * cov
            else:
                square = square + 2.0 * (cov * cov)
            b[at(i), at(j)] = cov
    trace = jnp.sum(trace, axis=(0, 1), keepdims=True)
    square = jnp.sum(square, axis=(0, 1), keepdims=True)
    ridge = 0.05 * trace / width + 1e-06
    norm = jnp.sqrt(square + 2.0 * ridge * trace + width * ridge * ridge)
    inv_norm = 1.0 / norm

    def put(value, i, j, high, low):
        h, l = split(value)
        high[at(i), at(j)] = h
        low[at(i), at(j)] = l
        if i != j:
            h, l = split(value.T)
            high[at(j), at(i)] = h
            low[at(j), at(i)] = l

    for i in range(NB):
        for j in range(i, NB):
            value = b[at(i), at(j)]
            if i == j:
                value = value + ridge * eye
            value = value * inv_norm
            b[at(i), at(j)] = value
            put(value, i, j, bh, bl)

    step = 2 * BLK

    def square_of(p, high, low):
        take, rest = slice(p * step, (p + 1) * step), slice(p * step, width)
        return (
            jnp.dot(high[take, :], high[:, rest], preferred_element_type=F32)
            + jnp.dot(high[take, :], low[:, rest], preferred_element_type=F32)
            + jnp.dot(low[take, :], high[:, rest], preferred_element_type=F32)
        )

    def blocks(p, panel):
        for i in (2 * p, 2 * p + 1):
            for j in range(i, NB):
                r, c = i - 2 * p, j - 2 * p
                yield i, j, panel[r * BLK:(r + 1) * BLK, c * BLK:(c + 1) * BLK]

    for p in range(NB // 2):
        for i, j, value in blocks(p, square_of(p, bh, bl)):
            own = b[at(i), at(j)]
            put(value - 4.5 * own, i, j, sh, sl)
            value = 6.75 * value - 39.0 * own
            b2[at(i), at(j)] = value + 36.0 * eye if i == j else value
    scale = lax.rsqrt(norm) / 16.0
    for p in range(NB // 2):
        for i, j, value in blocks(p, square_of(p, sh, sl)):
            put((value + b2[at(i), at(j)]) * scale, i, j, bh, bl)

    line = jnp.concatenate([center[i:i + 1, :] for i in range(NB)], axis=1)
    c_high = line.astype(BF16).astype(F32)
    c_mid = (line - c_high).astype(BF16).astype(F32)
    c_low = line - c_high - c_mid
    which = lax.broadcasted_iota(jnp.int32, (16, width), 0)
    x_ref[n_rows:n_rows + 16, :] = jnp.where(
        which == 0, c_high,
        jnp.where(which == 1, c_mid, jnp.where(which == 2, c_low, 0.0)),
    ).astype(BF16)
    load.wait()
    stores = []
    for k in range(width // step):
        cols = slice(k * step, (k + 1) * step)
        value = jnp.dot(x_ref[...], bh[:, cols], preferred_element_type=F32) + jnp.dot(
            x_ref[...], bl[:, cols], preferred_element_type=F32
        )
        shift = jnp.sum(value[n_rows:, :], axis=0, keepdims=True)
        o_ref[:, cols] = (value[:n_rows, :] - shift).astype(BF16)
        cols = pl.ds(k * step, step)
        store = pltpu.make_async_copy(o_ref.at[:, cols], o_hbm.at[:, cols], store_sem.at[k])
        store.start()
        stores.append(store)
    for store in stores:
        store.wait()


def white(pooled, x):
    width = NB * BLK
    hbm = pl.BlockSpec(memory_space=pltpu.HBM)
    return pl.pallas_call(
        white_kernel,
        name="white",
        out_shape=jax.ShapeDtypeStruct(x.shape, BF16),
        in_specs=[pl.BlockSpec(memory_space=pltpu.VMEM), hbm],
        out_specs=hbm,
        scratch_shapes=[pltpu.VMEM((x.shape[0] + 16, width), BF16), pltpu.VMEM(x.shape, BF16)]
        + [pltpu.VMEM((width, width), F32)] * 2
        + [pltpu.VMEM((width, width), BF16)] * 4
        + [pltpu.SemaphoreType.DMA, pltpu.SemaphoreType.DMA((width // (2 * BLK),))],
        compiler_params=pltpu.CompilerParams(vmem_limit_bytes=48 * 2**20),
    )(pooled, x)


def on_device(embeddings, valid):
    return white(pool(embeddings, valid[None, :]), embeddings)


def solution(mesh):
    in_specs = (P(("wide", "narrow"), None), P(("wide", "narrow")))
    return jax.shard_map(
        on_device, mesh=mesh, in_specs=in_specs, out_specs=P(("wide", "narrow"), None), check_vma=False
    )
```

```python
import functools

import jax
import jax.numpy as jnp
from jax import lax
from jax.experimental import pallas as pl
from jax.experimental.pallas import tpu as pltpu
from jax.sharding import PartitionSpec as P

MESH = pl.DeviceIdType.MESH
F32 = jnp.float32
BF16 = jnp.bfloat16

SIZE = {"z": 8, "x": 4, "y": 8, "c": 2}
BLK = 128
NB = 8
HALF_ROWS = ((0, 3, 4, 7), (1, 2, 5, 6))
A1X, A2X = 192, 128
AX = A1X + A2X
A1P, A2P = A1X // 8, A2X // 8
BY, BX = 64, 16
B0 = 4 * AX
C0 = B0 + 8 * BY
D0 = C0 + 8 * BY
HALF = D0 + 8
GX = AX + 8
GB = 4 * GX
GC = GB + 8 * BY
GHALF = GC + 8 * BY
N_COPIES = 120
FAR_8 = (4, 3, 5, 2, 6, 1, 7)
FAR_4 = (2, 1, 3)


def block_place(i, j):
    half = 0 if i in HALF_ROWS[0] else 1
    row = 0
    for k in HALF_ROWS[half]:
        if k == i:
            break
        row += NB - k
    return half, (row + j - i) * BLK


def coords():
    w, n = lax.axis_index("wide"), lax.axis_index("narrow")
    return {"z": w // 4, "x": w % 4, "y": n // 2, "c": n % 2}


def moved(me, axis, step):
    at = dict(me)
    at[axis] = lax.rem(me[axis] + step + SIZE[axis], SIZE[axis])
    return at


def ident(at):
    return (at["z"] * 4 + at["x"], at["y"] * 2 + at["c"])


def order(axis):
    return {"x": FAR_4, "y": FAR_8, "z": FAR_8, "c": (1,)}[axis]


def rows(start, size):
    return pl.ds(pl.multiple_of(start, 8), size)


def summed_row(row):
    return row // AX * GX + row % AX if row < B0 else row - B0 + GB


def total(own, parts):
    value = own
    for k in range(parts.shape[0]):
        value = value + parts[k]
    return value


def pool_kernel(
    x_hbm, valid_hbm, out_ref,
    x_ref, valid_ref, g, got, acc,
    r1x, r1y, r1z, s1a, s1e, s1x, r2x, r2y, r2z, s2z, s2y, r3z, r3y,
    load_sem, send_sem, recv_sem,
):
    me = coords()
    core = me["c"]
    barrier = pltpu.get_barrier_semaphore()
    count = 0
    for axis in ("z", "y", "x", "c"):
        for step in order(axis):
            pl.semaphore_signal(
                barrier, inc=1, device_id=ident(moved(me, axis, step)), device_id_type=MESH
            )
            count += 1
    loads = [
        pltpu.make_async_copy(x_hbm, x_ref, load_sem.at[0]),
        pltpu.make_async_copy(valid_hbm, valid_ref, load_sem.at[1]),
    ]
    for load in loads:
        load.start()
    for load in loads:
        load.wait()

    mask = valid_ref[...].astype(F32)
    mask_half = mask.astype(BF16)
    for half in range(2):
        for i in HALF_ROWS[half]:
            left = x_ref[:, i * BLK:(i + 1) * BLK].T * mask_half
            panel = jnp.dot(left, x_ref[:, i * BLK:], preferred_element_type=F32)
            for j in range(i, NB):
                _, row = block_place(i, j)
                for k in range(0, BLK, 64):
                    to = summed_row(row + k)
                    g[half, to:to + 64, :] = panel[k:k + 64, (j - i) * BLK:(j - i + 1) * BLK]
    sums = jnp.dot(
        jnp.broadcast_to(mask_half, (16, mask.shape[1])), x_ref[...], preferred_element_type=F32
    )
    valid_count = jnp.broadcast_to(jnp.sum(mask, axis=1, keepdims=True), (8, BLK))
    for part in range(4):
        to = part * GX + AX
        for i in range(NB):
            g[0, to + i:to + i + 1, :] = sums[0:1, i * BLK:(i + 1) * BLK]
        g[1, to:to + 8, :] = valid_count

    pl.semaphore_wait(barrier, count)

    used = []

    def copy(src, dst, axis, step):
        at = len(used)
        made = pltpu.make_async_remote_copy(
            src_ref=src, dst_ref=dst, send_sem=send_sem.at[at], recv_sem=recv_sem.at[at],
            device_id=ident(moved(me, axis, step)), device_id_type=MESH,
        )
        used.append(made)
        made.start()
        return made

    def arrive(copies):
        for made in copies:
            made.wait_recv()

    def beside(axis, step):
        return moved(me, axis, step)[axis]

    cuts = [pl.ds(GB, GHALF - GB)] + [rows(GX * beside("x", s), GX) for s in FAR_4 + (0,)]
    pair = [copy(g.at[1 - core, cut], got.at[cut], "c", 1) for cut in cuts]

    def add_pair(k):
        pair[k].wait_recv()
        acc[cuts[k], :] = g[core, cuts[k], :] + got[cuts[k], :]

    add_pair(0)
    w1y, w1z = [], []
    for s in FAR_8:
        w1y.append(copy(acc.at[rows(GB + BY * beside("y", s), BY)], r1y.at[s - 1], "y", s))
        w1z.append(copy(acc.at[rows(GC + BY * beside("z", s), BY)], r1z.at[s - 1], "z", s))
    w1x = []
    for k, s in enumerate(FAR_4):
        add_pair(k + 1)
        w1x.append(copy(acc.at[cuts[k + 1]], r1x.at[s - 1], "x", s))
    add_pair(4)

    arrive(w1x)
    s1a[...] = total(acc[rows(GX * me["x"], GX), :], r1x)
    w2y = [copy(s1a.at[rows(A1P * beside("y", s), A1P)], r2y.at[s - 1], "y", s) for s in FAR_8]
    for k in range(8):
        s1e[k, 0:A2P, :] = s1a[A1X + A2P * k:A1X + A2P * (k + 1), :]
        s1e[k, A2P:A2P + 8, :] = s1a[AX:GX, :]
    w2z = [copy(s1e.at[beside("z", s)], r2z.at[s - 1], "z", s) for s in FAR_8]
    arrive(w1y)
    value = total(acc[rows(GB + BY * me["y"], BY), :], r1y)
    for k in range(4):
        s1x[k, 0:BX, :] = value[BX * k:BX * (k + 1), :]
    arrive(w1z)
    value = total(acc[rows(GC + BY * me["z"], BY), :], r1z)
    for k in range(4):
        s1x[k, BX:2 * BX, :] = value[BX * k:BX * (k + 1), :]
    w2x = [copy(s1x.at[beside("x", s)], r2x.at[s - 1], "x", s) for s in FAR_4]

    arrive(w2y)
    s2z[0:A1P, :] = total(s1a[rows(A1P * me["y"], A1P), :], r2y)
    arrive(w2x)
    value = total(s1x[me["x"]], r2x)
    s2z[A1P:A1P + BX, :] = value[0:BX, :]
    w3z = [copy(s2z, r3z.at[s - 1], "z", s) for s in FAR_8]
    s2y[A2P + 8:A2P + 8 + BX, :] = value[BX:2 * BX, :]
    arrive(w2z)
    s2y[0:A2P + 8, :] = total(s1e[me["z"]], r2z)
    w3y = [copy(s2y, r3y.at[s - 1], "y", s) for s in FAR_8]

    def share(start, size, axis):
        piece = out_ref.at[core, rows(start, size)]
        return [copy(piece, piece, axis, s) for s in order(axis)]

    ax = AX * me["x"]
    a_at, e_at = ax + A1P * me["y"], ax + A1X + A2P * me["z"]
    b_at, c_at = B0 + BY * me["y"], C0 + BY * me["z"]
    arrive(w3z)
    value = total(s2z[...], r3z)
    out_ref[core, rows(b_at + BX * me["x"], BX), :] = value[A1P:A1P + BX, :]
    w4b = share(b_at + BX * me["x"], BX, "x")
    out_ref[core, rows(a_at, A1P), :] = value[0:A1P, :]
    w4a = share(a_at, A1P, "y")
    arrive(w3y)
    value = total(s2y[...], r3y)
    out_ref[core, rows(c_at + BX * me["x"], BX), :] = value[A2P + 8:A2P + 8 + BX, :]
    w4c = share(c_at + BX * me["x"], BX, "x")
    out_ref[core, rows(e_at, A2P), :] = value[0:A2P, :]
    w4e = share(e_at, A2P, "z")
    out_ref[core, D0:HALF, :] = value[A2P:A2P + 8, :]

    arrive(w4b)
    w5b = share(b_at, BY, "y")
    arrive(w4c)
    w5c = share(c_at, BY, "z")
    arrive(w4a)
    w5a = share(ax, A1X, "x")
    arrive(w4e)
    w5e = share(ax + A1X, A2X, "x")
    w6 = share(D0, 8, "c") + share(ax, AX, "c") + share(b_at, BY, "c") + share(c_at, BY, "c")
    for s in (1, 7, 2, 6, 3, 5, 4):
        k = FAR_8.index(s)
        w5b[k].wait_recv()
        w6 += share(B0 + BY * beside("y", -s), BY, "c")
        w5c[k].wait_recv()
        w6 += share(C0 + BY * beside("z", -s), BY, "c")
        if s in (7, 6, 5):
            k = (7, 6, 5).index(s)
            s = (1, 3, 2)[k]
            k = FAR_4.index(s)
            w5a[k].wait_recv()
            w5e[k].wait_recv()
            w6 += share(AX * beside("x", -s), AX, "c")
    arrive(w6)
    for made in used:
        made.wait_send()


def pool(x, valid):
    part = lambda n, r: pltpu.VMEM((n, r, BLK), F32)
    flat = lambda r: pltpu.VMEM((r, BLK), F32)
    return pl.pallas_call(
        pool_kernel,
        name="pool",
        out_shape=jax.ShapeDtypeStruct((2, HALF, BLK), F32),
        in_specs=[pl.BlockSpec(memory_space=pltpu.HBM)] * 2,
        out_specs=pl.BlockSpec(memory_space=pltpu.VMEM),
        scratch_shapes=[
            pltpu.VMEM(x.shape, BF16), pltpu.VMEM(valid.shape, jnp.int32),
            part(2, GHALF), flat(GHALF), flat(GHALF),
            part(3, GX), part(7, BY), part(7, BY),
            flat(GX), part(8, A2P + 8), part(4, 2 * BX),
            part(3, 2 * BX), part(7, A1P), part(7, A2P + 8),
            flat(A1P + BX), flat(A2P + 8 + BX), part(7, A1P + BX), part(7, A2P + 8 + BX),
            pltpu.SemaphoreType.DMA((2,)),
            pltpu.SemaphoreType.DMA((N_COPIES,)), pltpu.SemaphoreType.DMA((N_COPIES,)),
        ],
        compiler_params=pltpu.CompilerParams(
            collective_id=0, has_side_effects=True, vmem_limit_bytes=40 * 2**20
        ),
    )(x, valid)


def split(value):
    high = value.astype(BF16)
    return high, (value - high.astype(F32)).astype(BF16)


def white_kernel(f_ref, x_hbm, o_hbm, x_ref, o_ref, b, hh, hl, bh, bl, sh, sl, load_sem, store_sem):
    width = NB * BLK
    n_rows = x_hbm.shape[0]
    load = pltpu.make_async_copy(x_hbm, x_ref.at[pl.ds(0, n_rows)], load_sem)
    load.start()
    count = f_ref[1, D0:D0 + 1, :]
    inverse = 1.0 / count
    sums = f_ref[0, D0:D0 + 8, :]
    center = sums / count
    diag = (
        lax.broadcasted_iota(jnp.int32, (BLK, BLK), 0)
        == lax.broadcasted_iota(jnp.int32, (BLK, BLK), 1)
    )
    eye = diag.astype(F32)

    def at(i):
        return slice(i * BLK, (i + 1) * BLK)

    def put(value, i, j, high, low):
        h, l = split(value)
        high[at(i), at(j)] = h
        low[at(i), at(j)] = l
        if i != j:
            h, l = split(value.T)
            high[at(j), at(i)] = h
            low[at(j), at(i)] = l

    trace = jnp.zeros((BLK, BLK), F32)
    square = jnp.zeros((BLK, BLK), F32)
    for i in range(NB):
        column = jnp.broadcast_to(sums[i:i + 1, :], (BLK, BLK)).T
        for j in range(i, NB):
            half, row = block_place(i, j)
            scatter = f_ref[half, row:row + BLK, :] - column * center[j:j + 1, :]
            cov = scatter * inverse
            if i == j:
                trace = trace + jnp.where(diag, cov, 0.0)
                square = square + cov * cov
            else:
                square = square + 2.0 * (cov * cov)
            b[at(i), at(j)] = cov
            put(cov, i, j, bh, bl)

    step = 2 * BLK

    def squared(high, low, use):
        for p in range(NB // 2):
            take, rest = slice(p * step, (p + 1) * step), slice(p * step, width)
            hh[take, rest] = jnp.dot(high[take, :], high[:, rest], preferred_element_type=F32)
            hl[take, :] = jnp.dot(high[take, :], low[...], preferred_element_type=F32)
            for j in (2 * p, 2 * p + 1):
                for i in range(j + 1):
                    use(i, j, hh[at(i), at(j)] + (hl[at(i), at(j)] + hl[at(j), at(i)].T))

    trace = jnp.sum(trace, axis=(0, 1), keepdims=True)
    square = jnp.sum(square, axis=(0, 1), keepdims=True)
    ridge = 0.05 * trace / width + 1e-06
    norm = jnp.sqrt(square + 2.0 * ridge * trace + width * ridge * ridge)
    inv_norm = 1.0 / norm
    inv_norm2 = inv_norm * inv_norm
    scale = lax.rsqrt(norm) / 16.0

    def half_way(i, j, value):
        cov = b[at(i), at(j)]
        value = value + (2.0 * ridge) * cov
        if i == j:
            value = value + (ridge * ridge) * eye
            cov = cov + ridge * eye
        base, base2 = cov * inv_norm, value * inv_norm2
        put(base2 - 4.5 * base, i, j, sh, sl)
        rest = 6.75 * base2 - 39.0 * base
        b[at(i), at(j)] = rest + 36.0 * eye if i == j else rest

    def rooted(i, j, value):
        put((value + b[at(i), at(j)]) * scale, i, j, bh, bl)

    squared(bh, bl, half_way)
    squared(sh, sl, rooted)

    line = jnp.concatenate([center[i:i + 1, :] for i in range(NB)], axis=1)
    c_high = line.astype(BF16).astype(F32)
    c_mid = (line - c_high).astype(BF16).astype(F32)
    c_low = line - c_high - c_mid
    which = lax.broadcasted_iota(jnp.int32, (16, width), 0)
    x_ref[n_rows:n_rows + 16, :] = jnp.where(
        which == 0, c_high,
        jnp.where(which == 1, c_mid, jnp.where(which == 2, c_low, 0.0)),
    ).astype(BF16)
    load.wait()
    stores = []
    for k in range(width // step):
        cols = slice(k * step, (k + 1) * step)
        value = jnp.dot(x_ref[...], bh[:, cols], preferred_element_type=F32) + jnp.dot(
            x_ref[...], bl[:, cols], preferred_element_type=F32
        )
        shift = jnp.sum(value[n_rows:, :], axis=0, keepdims=True)
        o_ref[:, cols] = (value[:n_rows, :] - shift).astype(BF16)
        cols = pl.ds(k * step, step)
        store = pltpu.make_async_copy(o_ref.at[:, cols], o_hbm.at[:, cols], store_sem.at[k])
        store.start()
        stores.append(store)
    for store in stores:
        store.wait()


def white(pooled, x):
    width = NB * BLK
    hbm = pl.BlockSpec(memory_space=pltpu.HBM)
    return pl.pallas_call(
        white_kernel,
        name="white",
        out_shape=jax.ShapeDtypeStruct(x.shape, BF16),
        in_specs=[pl.BlockSpec(memory_space=pltpu.VMEM), hbm],
        out_specs=hbm,
        scratch_shapes=[pltpu.VMEM((x.shape[0] + 16, width), BF16), pltpu.VMEM(x.shape, BF16)]
        + [pltpu.VMEM((width, width), F32)] * 3
        + [pltpu.VMEM((width, width), BF16)] * 4
        + [pltpu.SemaphoreType.DMA, pltpu.SemaphoreType.DMA((width // (2 * BLK),))],
        compiler_params=pltpu.CompilerParams(vmem_limit_bytes=48 * 2**20),
    )(pooled, x)


def on_device(embeddings, valid):
    embeddings = pltpu.with_memory_space_constraint(embeddings, pltpu.HBM)
    valid = pltpu.with_memory_space_constraint(valid[None, :], pltpu.HBM)
    return white(pool(embeddings, valid), embeddings)


def solution(mesh):
    in_specs = (P(("wide", "narrow"), None), P(("wide", "narrow")))
    return jax.shard_map(
        on_device, mesh=mesh, in_specs=in_specs, out_specs=P(("wide", "narrow"), None), check_vma=False
    )
```

```python
import functools

import jax
import jax.numpy as jnp
from jax import lax
from jax.experimental import pallas as pl
from jax.experimental.pallas import tpu as pltpu
from jax.sharding import PartitionSpec as P

MESH = pl.DeviceIdType.MESH
F32 = jnp.float32
BF16 = jnp.bfloat16

SIZE = {"z": 8, "x": 4, "y": 8, "c": 2}
BLK = 128
NB = 8
HALF_ROWS = ((0, 3, 4, 7), (1, 2, 5, 6))
A1X, A2X = 128, 128
AX = A1X + A2X
A1P, A2P = A1X // 8, A2X // 8
BY, BX = 80, 24
BS = 4 * BX
B0 = 4 * AX
C0 = B0 + 8 * BS
D0 = C0 + 8 * BS
HALF = D0 + 8
GX = AX + 8
GB = 4 * GX
GC = GB + 8 * BY
GHALF = GC + 8 * BY
N_COPIES = 120
FAR_8 = (4, 3, 5, 2, 6, 1, 7)
FAR_4 = (2, 1, 3)


def block_place(i, j):
    half = 0 if i in HALF_ROWS[0] else 1
    row = 0
    for k in HALF_ROWS[half]:
        if k == i:
            break
        row += NB - k
    return half, (row + j - i) * BLK


def coords():
    w, n = lax.axis_index("wide"), lax.axis_index("narrow")
    return {"z": w // 4, "x": w % 4, "y": n // 2, "c": n % 2}


def moved(me, axis, step):
    at = dict(me)
    at[axis] = lax.rem(me[axis] + step + SIZE[axis], SIZE[axis])
    return at


def ident(at):
    return (at["z"] * 4 + at["x"], at["y"] * 2 + at["c"])


def order(axis):
    return {"x": FAR_4, "y": FAR_8, "z": FAR_8, "c": (1,)}[axis]


def rows(start, size):
    return pl.ds(pl.multiple_of(start, 8), size)


def summed_row(row):
    return row // AX * GX + row % AX if row < B0 else row - B0 + GB


def result_row(row):
    if row < B0:
        return row
    place, row = divmod(row - B0, BY)
    return B0 + place * BS + row


def runs(row, where):
    found = []
    for k in range(0, BLK, 16):
        to = where(row + k)
        if found and found[-1][1] + found[-1][2] == to:
            found[-1][2] += 16
        else:
            found.append([k, to, 16])
    return found


def total(own, parts):
    value = own
    for k in range(parts.shape[0]):
        value = value + parts[k]
    return value


def pool_kernel(
    x_hbm, valid_hbm, out_ref,
    x_ref, valid_ref, g, got, acc,
    r1x, r1y, r1z, s1a, s1e, s1x, r2x, r2y, r2z, s2z, s2y, r3z, r3y,
    load_sem, send_sem, recv_sem,
):
    me = coords()
    core = me["c"]
    barrier = pltpu.get_barrier_semaphore()
    count = 0
    for axes in ("zy", "x", "c"):
        for step in order(axes[0]):
            for axis in axes:
                pl.semaphore_signal(
                    barrier, inc=1, device_id=ident(moved(me, axis, step)), device_id_type=MESH
                )
                count += 1
    loads = [
        pltpu.make_async_copy(x_hbm, x_ref, load_sem.at[0]),
        pltpu.make_async_copy(valid_hbm, valid_ref, load_sem.at[1]),
    ]
    for load in loads:
        load.start()
    for load in loads:
        load.wait()

    mask = valid_ref[...].astype(F32)
    mask_half = mask.astype(BF16)
    for half in range(2):
        for i in HALF_ROWS[half]:
            left = x_ref[:, i * BLK:(i + 1) * BLK].T * mask_half
            panel = jnp.dot(left, x_ref[:, i * BLK:], preferred_element_type=F32)
            for j in range(i, NB):
                _, row = block_place(i, j)
                for k, to, n in runs(row, summed_row):
                    g[half, to:to + n, :] = panel[k:k + n, (j - i) * BLK:(j - i + 1) * BLK]
    sums = jnp.dot(
        jnp.broadcast_to(mask_half, (16, mask.shape[1])), x_ref[...], preferred_element_type=F32
    )
    valid_count = jnp.broadcast_to(jnp.sum(mask, axis=1, keepdims=True), (8, BLK))
    for part in range(4):
        to = part * GX + AX
        for i in range(NB):
            g[0, to + i:to + i + 1, :] = sums[0:1, i * BLK:(i + 1) * BLK]
        g[1, to:to + 8, :] = valid_count

    pl.semaphore_wait(barrier, count)

    used = []

    def copy(src, dst, axis, step):
        at = len(used)
        made = pltpu.make_async_remote_copy(
            src_ref=src, dst_ref=dst, send_sem=send_sem.at[at], recv_sem=recv_sem.at[at],
            device_id=ident(moved(me, axis, step)), device_id_type=MESH,
        )
        used.append(made)
        made.start()
        return made

    def arrive(copies):
        for made in copies:
            made.wait_recv()

    def beside(axis, step):
        return moved(me, axis, step)[axis]

    cuts = [pl.ds(GB, 8 * BY), pl.ds(GC, 8 * BY)]
    cuts += [rows(GX * beside("x", s), GX) for s in FAR_4 + (0,)]
    pair = [copy(g.at[1 - core, cut], got.at[cut], "c", 1) for cut in cuts]

    def add_pair(k):
        pair[k].wait_recv()
        acc[cuts[k], :] = g[core, cuts[k], :] + got[cuts[k], :]

    add_pair(0)
    w1y = [copy(acc.at[rows(GB + BY * beside("y", s), BY)], r1y.at[s - 1], "y", s) for s in FAR_8]
    add_pair(1)
    w1z = [copy(acc.at[rows(GC + BY * beside("z", s), BY)], r1z.at[s - 1], "z", s) for s in FAR_8]
    w1x = []
    for k, s in enumerate(FAR_4):
        add_pair(k + 2)
        w1x.append(copy(acc.at[cuts[k + 2]], r1x.at[s - 1], "x", s))
    add_pair(5)

    def quarters(value, first):
        for k in range(4):
            n = min(BX, BY - BX * k)
            s1x[k, first:first + n, :] = value[BX * k:BX * k + n, :]
            if n < BX:
                s1x[k, first + n:first + BX, :] = jnp.zeros((BX - n, BLK), F32)

    arrive(w1x)
    s1a[...] = total(acc[rows(GX * me["x"], GX), :], r1x)
    w2y = [copy(s1a.at[rows(A1P * beside("y", s), A1P)], r2y.at[s - 1], "y", s) for s in FAR_8]
    for k in range(8):
        s1e[k, 0:A2P, :] = s1a[A1X + A2P * k:A1X + A2P * (k + 1), :]
        s1e[k, A2P:A2P + 8, :] = s1a[AX:GX, :]
    w2z = [copy(s1e.at[beside("z", s)], r2z.at[s - 1], "z", s) for s in FAR_8]
    arrive(w1y)
    quarters(total(acc[rows(GB + BY * me["y"], BY), :], r1y), 0)
    arrive(w1z)
    quarters(total(acc[rows(GC + BY * me["z"], BY), :], r1z), BX)
    w2x = [copy(s1x.at[beside("x", s)], r2x.at[s - 1], "x", s) for s in FAR_4]

    arrive(w2y)
    s2z[0:A1P, :] = total(s1a[rows(A1P * me["y"], A1P), :], r2y)
    arrive(w2x)
    value = total(s1x[me["x"]], r2x)
    s2z[A1P:A1P + BX, :] = value[0:BX, :]
    w3z = [copy(s2z, r3z.at[s - 1], "z", s) for s in FAR_8]
    s2y[A2P + 8:A2P + 8 + BX, :] = value[BX:2 * BX, :]
    arrive(w2z)
    s2y[0:A2P + 8, :] = total(s1e[me["z"]], r2z)
    w3y = [copy(s2y, r3y.at[s - 1], "y", s) for s in FAR_8]

    def share(start, size, axis):
        piece = out_ref.at[core, rows(start, size)]
        return [copy(piece, piece, axis, s) for s in order(axis)]

    ax = AX * me["x"]
    a_at, e_at = ax + A1P * me["y"], ax + A1X + A2P * me["z"]
    b_at, c_at = B0 + BS * me["y"], C0 + BS * me["z"]
    arrive(w3z)
    value = total(s2z[...], r3z)
    out_ref[core, rows(b_at + BX * me["x"], BX), :] = value[A1P:A1P + BX, :]
    w4b = share(b_at + BX * me["x"], BX, "x")
    out_ref[core, rows(a_at, A1P), :] = value[0:A1P, :]
    w4a = share(a_at, A1P, "y")
    arrive(w3y)
    value = total(s2y[...], r3y)
    out_ref[core, rows(c_at + BX * me["x"], BX), :] = value[A2P + 8:A2P + 8 + BX, :]
    w4c = share(c_at + BX * me["x"], BX, "x")
    out_ref[core, rows(e_at, A2P), :] = value[0:A2P, :]
    w4e = share(e_at, A2P, "z")
    out_ref[core, D0:HALF, :] = value[A2P:A2P + 8, :]

    arrive(w4b)
    w5b = share(b_at, BY, "y")
    arrive(w4c)
    w5c = share(c_at, BY, "z")
    arrive(w4a)
    w5a = share(ax, A1X, "x")
    arrive(w4e)
    w5e = share(ax + A1X, A2X, "x")
    w6 = share(D0, 8, "c") + share(ax, AX, "c") + share(b_at, BY, "c") + share(c_at, BY, "c")
    for s in (1, 7, 2, 6, 3, 5, 4):
        k = FAR_8.index(s)
        w5b[k].wait_recv()
        w6 += share(B0 + BS * beside("y", -s), BY, "c")
        w5c[k].wait_recv()
        w6 += share(C0 + BS * beside("z", -s), BY, "c")
        if s in (7, 6, 5):
            k = (7, 6, 5).index(s)
            s = (1, 3, 2)[k]
            k = FAR_4.index(s)
            w5a[k].wait_recv()
            w5e[k].wait_recv()
            w6 += share(AX * beside("x", -s), AX, "c")
    arrive(w6)
    for made in used:
        made.wait_send()


def pool(x, valid):
    part = lambda n, r: pltpu.VMEM((n, r, BLK), F32)
    flat = lambda r: pltpu.VMEM((r, BLK), F32)
    return pl.pallas_call(
        pool_kernel,
        name="pool",
        out_shape=jax.ShapeDtypeStruct((2, HALF, BLK), F32),
        in_specs=[pl.BlockSpec(memory_space=pltpu.HBM)] * 2,
        out_specs=pl.BlockSpec(memory_space=pltpu.VMEM),
        scratch_shapes=[
            pltpu.VMEM(x.shape, BF16), pltpu.VMEM(valid.shape, jnp.int32),
            part(2, GHALF), flat(GHALF), flat(GHALF),
            part(3, GX), part(7, BY), part(7, BY),
            flat(GX), part(8, A2P + 8), part(4, 2 * BX),
            part(3, 2 * BX), part(7, A1P), part(7, A2P + 8),
            flat(A1P + BX), flat(A2P + 8 + BX), part(7, A1P + BX), part(7, A2P + 8 + BX),
            pltpu.SemaphoreType.DMA((2,)),
            pltpu.SemaphoreType.DMA((N_COPIES,)), pltpu.SemaphoreType.DMA((N_COPIES,)),
        ],
        compiler_params=pltpu.CompilerParams(
            collective_id=0, has_side_effects=True, vmem_limit_bytes=40 * 2**20
        ),
    )(x, valid)


def split(value):
    high = value.astype(BF16)
    return high, (value - high.astype(F32)).astype(BF16)


def white_kernel(f_ref, x_hbm, o_hbm, x_ref, o_ref, b, hh, hl, bh, bl, sh, sl, load_sem, store_sem):
    width = NB * BLK
    n_rows = x_hbm.shape[0]
    load = pltpu.make_async_copy(x_hbm, x_ref.at[pl.ds(0, n_rows)], load_sem)
    load.start()
    count = f_ref[1, D0:D0 + 1, :]
    inverse = 1.0 / count
    sums = f_ref[0, D0:D0 + 8, :]
    center = sums / count
    diag = (
        lax.broadcasted_iota(jnp.int32, (BLK, BLK), 0)
        == lax.broadcasted_iota(jnp.int32, (BLK, BLK), 1)
    )
    eye = diag.astype(F32)

    def at(i):
        return slice(i * BLK, (i + 1) * BLK)

    def put(value, i, j, high, low):
        h, l = split(value)
        high[at(i), at(j)] = h
        low[at(i), at(j)] = l
        if i != j:
            h, l = split(value.T)
            high[at(j), at(i)] = h
            low[at(j), at(i)] = l

    trace = jnp.zeros((BLK, BLK), F32)
    square = jnp.zeros((BLK, BLK), F32)
    for i in range(NB):
        column = jnp.broadcast_to(sums[i:i + 1, :], (BLK, BLK)).T
        for j in range(i, NB):
            half, row = block_place(i, j)
            pooled = jnp.concatenate(
                [f_ref[half, to:to + n, :] for _, to, n in runs(row, result_row)], axis=0
            )
            scatter = pooled - column * center[j:j + 1, :]
            cov = scatter * inverse
            if i == j:
                trace = trace + jnp.where(diag, cov, 0.0)
                square = square + cov * cov
            else:
                square = square + 2.0 * (cov * cov)
            b[at(i), at(j)] = cov
            put(cov, i, j, bh, bl)

    step = 2 * BLK

    def squared(high, low, use):
        for p in range(NB // 2):
            take, rest = slice(p * step, (p + 1) * step), slice(p * step, width)
            hh[take, rest] = jnp.dot(high[take, :], high[:, rest], preferred_element_type=F32)
            hl[take, :] = jnp.dot(high[take, :], low[...], preferred_element_type=F32)
            for j in (2 * p, 2 * p + 1):
                for i in range(j + 1):
                    use(i, j, hh[at(i), at(j)] + (hl[at(i), at(j)] + hl[at(j), at(i)].T))

    trace = jnp.sum(trace, axis=(0, 1), keepdims=True)
    square = jnp.sum(square, axis=(0, 1), keepdims=True)
    ridge = 0.05 * trace / width + 1e-06
    norm = jnp.sqrt(square + 2.0 * ridge * trace + width * ridge * ridge)
    inv_norm = 1.0 / norm
    inv_norm2 = inv_norm * inv_norm
    scale = lax.rsqrt(norm) / 16.0

    def half_way(i, j, value):
        cov = b[at(i), at(j)]
        value = value + (2.0 * ridge) * cov
        if i == j:
            value = value + (ridge * ridge) * eye
            cov = cov + ridge * eye
        base, base2 = cov * inv_norm, value * inv_norm2
        put(base2 - 4.5 * base, i, j, sh, sl)
        rest = 6.75 * base2 - 39.0 * base
        b[at(i), at(j)] = rest + 36.0 * eye if i == j else rest

    def rooted(i, j, value):
        put((value + b[at(i), at(j)]) * scale, i, j, bh, bl)

    squared(bh, bl, half_way)
    squared(sh, sl, rooted)

    line = jnp.concatenate([center[i:i + 1, :] for i in range(NB)], axis=1)
    c_high = line.astype(BF16).astype(F32)
    c_mid = (line - c_high).astype(BF16).astype(F32)
    c_low = line - c_high - c_mid
    which = lax.broadcasted_iota(jnp.int32, (16, width), 0)
    x_ref[n_rows:n_rows + 16, :] = jnp.where(
        which == 0, c_high,
        jnp.where(which == 1, c_mid, jnp.where(which == 2, c_low, 0.0)),
    ).astype(BF16)
    load.wait()
    stores = []
    for k in range(width // step):
        cols = slice(k * step, (k + 1) * step)
        value = jnp.dot(x_ref[...], bh[:, cols], preferred_element_type=F32) + jnp.dot(
            x_ref[...], bl[:, cols], preferred_element_type=F32
        )
        shift = jnp.sum(value[n_rows:, :], axis=0, keepdims=True)
        o_ref[:, cols] = (value[:n_rows, :] - shift).astype(BF16)
        cols = pl.ds(k * step, step)
        store = pltpu.make_async_copy(o_ref.at[:, cols], o_hbm.at[:, cols], store_sem.at[k])
        store.start()
        stores.append(store)
    for store in stores:
        store.wait()


def white(pooled, x):
    width = NB * BLK
    hbm = pl.BlockSpec(memory_space=pltpu.HBM)
    return pl.pallas_call(
        white_kernel,
        name="white",
        out_shape=jax.ShapeDtypeStruct(x.shape, BF16),
        in_specs=[pl.BlockSpec(memory_space=pltpu.VMEM), hbm],
        out_specs=hbm,
        scratch_shapes=[pltpu.VMEM((x.shape[0] + 16, width), BF16), pltpu.VMEM(x.shape, BF16)]
        + [pltpu.VMEM((width, width), F32)] * 3
        + [pltpu.VMEM((width, width), BF16)] * 4
        + [pltpu.SemaphoreType.DMA, pltpu.SemaphoreType.DMA((width // (2 * BLK),))],
        compiler_params=pltpu.CompilerParams(vmem_limit_bytes=48 * 2**20),
    )(pooled, x)


def on_device(embeddings, valid):
    embeddings = pltpu.with_memory_space_constraint(embeddings, pltpu.HBM)
    valid = pltpu.with_memory_space_constraint(valid[None, :], pltpu.HBM)
    return white(pool(embeddings, valid), embeddings)


def solution(mesh):
    in_specs = (P(("wide", "narrow"), None), P(("wide", "narrow")))
    return jax.shard_map(
        on_device, mesh=mesh, in_specs=in_specs, out_specs=P(("wide", "narrow"), None), check_vma=False
    )
```

```python
import functools

import jax
import jax.numpy as jnp
from jax import lax
from jax.experimental import pallas as pl
from jax.experimental.pallas import tpu as pltpu
from jax.sharding import PartitionSpec as P

MESH = pl.DeviceIdType.MESH
F32 = jnp.float32
BF16 = jnp.bfloat16

SIZE = {"z": 8, "x": 4, "y": 8, "c": 2}
BLK = 128
NB = 8
HALF_ROWS = ((0, 3, 4, 7), (1, 2, 5, 6))
A1X, A2X = 128, 128
AX = A1X + A2X
A1P, A2P = A1X // 8, A2X // 8
BY, BX = 80, 24
BS = 4 * BX
B0 = 4 * AX
C0 = B0 + 8 * BS
D0 = C0 + 8 * BS
HALF = D0 + 8
GX = AX + 8
GB = 4 * GX
GC = GB + 8 * BY
GHALF = GC + 8 * BY
N_COPIES = 120
FAR_8 = (4, 3, 5, 2, 6, 1, 7)
FAR_4 = (2, 1, 3)


def block_place(i, j):
    half = 0 if i in HALF_ROWS[0] else 1
    row = 0
    for k in HALF_ROWS[half]:
        if k == i:
            break
        row += NB - k
    return half, (row + j - i) * BLK


def coords():
    w, n = lax.axis_index("wide"), lax.axis_index("narrow")
    return {"z": w // 4, "x": w % 4, "y": n // 2, "c": n % 2}


def moved(me, axis, step):
    at = dict(me)
    at[axis] = lax.rem(me[axis] + step + SIZE[axis], SIZE[axis])
    return at


def ident(at):
    return (at["z"] * 4 + at["x"], at["y"] * 2 + at["c"])


def order(axis):
    return {"x": FAR_4, "y": FAR_8, "z": FAR_8, "c": (1,)}[axis]


def rows(start, size):
    return pl.ds(pl.multiple_of(start, 8), size)


def summed_row(row):
    return row // AX * GX + row % AX if row < B0 else row - B0 + GB


def result_row(row):
    if row < B0:
        return row
    place, row = divmod(row - B0, BY)
    return B0 + place * BS + row


def runs(row, where):
    found = []
    for k in range(0, BLK, 16):
        to = where(row + k)
        if found and found[-1][1] + found[-1][2] == to:
            found[-1][2] += 16
        else:
            found.append([k, to, 16])
    return found


def total(own, parts):
    value = own
    for k in range(parts.shape[0]):
        value = value + parts[k]
    return value


def pool_kernel(
    x_hbm, valid_hbm, out_ref,
    x_ref, valid_ref, g, got, acc,
    r1x, r1y, r1z, s1a, s1e, s1x, r2x, r2y, r2z, s2z, s2y, r3z, r3y,
    load_sem, send_sem, recv_sem,
):
    me = coords()
    core = me["c"]
    barrier = pltpu.get_barrier_semaphore()
    count = 0
    for axes in ("zy", "x", "c"):
        for step in order(axes[0]):
            for axis in axes:
                pl.semaphore_signal(
                    barrier, inc=1, device_id=ident(moved(me, axis, step)), device_id_type=MESH
                )
                count += 1
    loads = [
        pltpu.make_async_copy(x_hbm, x_ref, load_sem.at[0]),
        pltpu.make_async_copy(valid_hbm, valid_ref, load_sem.at[1]),
    ]
    for load in loads:
        load.start()
    for load in loads:
        load.wait()

    mask = valid_ref[...].astype(F32)
    mask_half = mask.astype(BF16)
    for half in range(2):
        for i in HALF_ROWS[half]:
            left = x_ref[:, i * BLK:(i + 1) * BLK].T * mask_half
            panel = jnp.dot(left, x_ref[:, i * BLK:], preferred_element_type=F32)
            for j in range(i, NB):
                _, row = block_place(i, j)
                for k, to, n in runs(row, summed_row):
                    g[half, to:to + n, :] = panel[k:k + n, (j - i) * BLK:(j - i + 1) * BLK]
    sums = jnp.dot(
        jnp.broadcast_to(mask_half, (16, mask.shape[1])), x_ref[...], preferred_element_type=F32
    )
    valid_count = jnp.broadcast_to(jnp.sum(mask, axis=1, keepdims=True), (8, BLK))
    for part in range(4):
        to = part * GX + AX
        for i in range(NB):
            g[0, to + i:to + i + 1, :] = sums[0:1, i * BLK:(i + 1) * BLK]
        g[1, to:to + 8, :] = valid_count

    pl.semaphore_wait(barrier, count)

    used = []

    def copy(src, dst, axis, step):
        at = len(used)
        made = pltpu.make_async_remote_copy(
            src_ref=src, dst_ref=dst, send_sem=send_sem.at[at], recv_sem=recv_sem.at[at],
            device_id=ident(moved(me, axis, step)), device_id_type=MESH,
        )
        used.append(made)
        made.start()
        return made

    def sent(copies):
        for made in copies:
            made.wait_send()

    def arrive(copies):
        for made in copies:
            made.wait_recv()

    def beside(axis, step):
        return moved(me, axis, step)[axis]

    cuts = [pl.ds(GB, 8 * BY), pl.ds(GC, 8 * BY)]
    cuts += [rows(GX * beside("x", s), GX) for s in FAR_4 + (0,)]
    pair = [copy(g.at[1 - core, cut], got.at[cut], "c", 1) for cut in cuts]

    def add_pair(k):
        pair[k].wait_recv()
        acc[cuts[k], :] = g[core, cuts[k], :] + got[cuts[k], :]

    add_pair(0)
    w1y = [copy(acc.at[rows(GB + BY * beside("y", s), BY)], r1y.at[s - 1], "y", s) for s in FAR_8]
    add_pair(1)
    w1z = [copy(acc.at[rows(GC + BY * beside("z", s), BY)], r1z.at[s - 1], "z", s) for s in FAR_8]
    w1x = []
    for k, s in enumerate(FAR_4):
        add_pair(k + 2)
        w1x.append(copy(acc.at[cuts[k + 2]], r1x.at[s - 1], "x", s))
    add_pair(5)

    def quarters(value, first):
        for k in range(4):
            n = min(BX, BY - BX * k)
            s1x[k, first:first + n, :] = value[BX * k:BX * k + n, :]
            if n < BX:
                s1x[k, first + n:first + BX, :] = jnp.zeros((BX - n, BLK), F32)

    arrive(w1x)
    s1a[...] = total(acc[rows(GX * me["x"], GX), :], r1x)
    w2y = [copy(s1a.at[rows(A1P * beside("y", s), A1P)], r2y.at[s - 1], "y", s) for s in FAR_8]
    for k in range(8):
        s1e[k, 0:A2P, :] = s1a[A1X + A2P * k:A1X + A2P * (k + 1), :]
        s1e[k, A2P:A2P + 8, :] = s1a[AX:GX, :]
    w2z = [copy(s1e.at[beside("z", s)], r2z.at[s - 1], "z", s) for s in FAR_8]
    arrive(w1y)
    quarters(total(acc[rows(GB + BY * me["y"], BY), :], r1y), 0)
    arrive(w1z)
    quarters(total(acc[rows(GC + BY * me["z"], BY), :], r1z), BX)
    w2x = [copy(s1x.at[beside("x", s)], r2x.at[s - 1], "x", s) for s in FAR_4]

    sent(pair)
    arrive(w2y)
    s2z[0:A1P, :] = total(s1a[rows(A1P * me["y"], A1P), :], r2y)
    arrive(w2x)
    value = total(s1x[me["x"]], r2x)
    s2z[A1P:A1P + BX, :] = value[0:BX, :]
    w3z = [copy(s2z, r3z.at[s - 1], "z", s) for s in FAR_8]
    s2y[A2P + 8:A2P + 8 + BX, :] = value[BX:2 * BX, :]
    arrive(w2z)
    s2y[0:A2P + 8, :] = total(s1e[me["z"]], r2z)
    w3y = [copy(s2y, r3y.at[s - 1], "y", s) for s in FAR_8]

    sent(w1y + w1z + w1x)
    def share(start, size, axis):
        piece = out_ref.at[core, rows(start, size)]
        return [copy(piece, piece, axis, s) for s in order(axis)]

    ax = AX * me["x"]
    a_at, e_at = ax + A1P * me["y"], ax + A1X + A2P * me["z"]
    b_at, c_at = B0 + BS * me["y"], C0 + BS * me["z"]
    arrive(w3z)
    value = total(s2z[...], r3z)
    out_ref[core, rows(b_at + BX * me["x"], BX), :] = value[A1P:A1P + BX, :]
    w4b = share(b_at + BX * me["x"], BX, "x")
    out_ref[core, rows(a_at, A1P), :] = value[0:A1P, :]
    w4a = share(a_at, A1P, "y")
    arrive(w3y)
    value = total(s2y[...], r3y)
    out_ref[core, rows(c_at + BX * me["x"], BX), :] = value[A2P + 8:A2P + 8 + BX, :]
    w4c = share(c_at + BX * me["x"], BX, "x")
    out_ref[core, rows(e_at, A2P), :] = value[0:A2P, :]
    w4e = share(e_at, A2P, "z")
    out_ref[core, D0:HALF, :] = value[A2P:A2P + 8, :]

    sent(w2x + w2y + w2z)
    arrive(w4b)
    w5b = share(b_at, BY, "y")
    arrive(w4c)
    w5c = share(c_at, BY, "z")
    arrive(w4a)
    w5a = share(ax, A1X, "x")
    arrive(w4e)
    w5e = share(ax + A1X, A2X, "x")
    w6 = share(D0, 8, "c") + share(ax, AX, "c") + share(b_at, BY, "c") + share(c_at, BY, "c")
    sent(w3z + w3y + w4b + w4c + w4a + w4e)
    for s in (1, 7, 2, 6, 3, 5, 4):
        k = FAR_8.index(s)
        w5b[k].wait_recv()
        w6 += share(B0 + BS * beside("y", -s), BY, "c")
        w5c[k].wait_recv()
        w6 += share(C0 + BS * beside("z", -s), BY, "c")
        if s in (7, 6, 5):
            k = (7, 6, 5).index(s)
            s = (1, 3, 2)[k]
            k = FAR_4.index(s)
            w5a[k].wait_recv()
            w5e[k].wait_recv()
            w6 += share(AX * beside("x", -s), AX, "c")
    sent(w5b + w5c + w5a + w5e)
    arrive(w6)
    sent(w6)


def pool(x, valid):
    part = lambda n, r: pltpu.VMEM((n, r, BLK), F32)
    flat = lambda r: pltpu.VMEM((r, BLK), F32)
    return pl.pallas_call(
        pool_kernel,
        name="pool",
        out_shape=jax.ShapeDtypeStruct((2, HALF, BLK), F32),
        in_specs=[pl.BlockSpec(memory_space=pltpu.HBM)] * 2,
        out_specs=pl.BlockSpec(memory_space=pltpu.VMEM),
        scratch_shapes=[
            pltpu.VMEM(x.shape, BF16), pltpu.VMEM(valid.shape, jnp.int32),
            part(2, GHALF), flat(GHALF), flat(GHALF),
            part(3, GX), part(7, BY), part(7, BY),
            flat(GX), part(8, A2P + 8), part(4, 2 * BX),
            part(3, 2 * BX), part(7, A1P), part(7, A2P + 8),
            flat(A1P + BX), flat(A2P + 8 + BX), part(7, A1P + BX), part(7, A2P + 8 + BX),
            pltpu.SemaphoreType.DMA((2,)),
            pltpu.SemaphoreType.DMA((N_COPIES,)), pltpu.SemaphoreType.DMA((N_COPIES,)),
        ],
        compiler_params=pltpu.CompilerParams(
            collective_id=0, has_side_effects=True, vmem_limit_bytes=40 * 2**20
        ),
    )(x, valid)


CHUNKS = ((0, 512), (512, 256), (768, 256))


def split(value):
    high = value.astype(BF16)
    return high, (value - high.astype(F32)).astype(BF16)


def white_kernel(f_ref, x_hbm, o_hbm, x_ref, o_ref, b, bh, bl, sh, sl, load_sem, store_sem):
    width = NB * BLK
    n_rows = x_hbm.shape[0]
    load = pltpu.make_async_copy(x_hbm, x_ref.at[pl.ds(0, n_rows)], load_sem)
    load.start()
    count = f_ref[1, D0:D0 + 1, :]
    inverse = 1.0 / count
    sums = f_ref[0, D0:D0 + 8, :]
    center = sums / count
    diag = (
        lax.broadcasted_iota(jnp.int32, (BLK, BLK), 0)
        == lax.broadcasted_iota(jnp.int32, (BLK, BLK), 1)
    )
    eye = diag.astype(F32)

    def at(i):
        return slice(i * BLK, (i + 1) * BLK)

    def put(value, i, j, high, low):
        h, l = split(value)
        high[at(i), at(j)] = h
        low[at(i), at(j)] = l
        if i != j:
            h, l = split(value.T)
            high[at(j), at(i)] = h
            low[at(j), at(i)] = l

    trace = jnp.zeros((BLK, BLK), F32)
    square = jnp.zeros((BLK, BLK), F32)
    for i in range(NB):
        column = jnp.broadcast_to(sums[i:i + 1, :], (BLK, BLK)).T
        for j in range(i, NB):
            half, row = block_place(i, j)
            pooled = jnp.concatenate(
                [f_ref[half, to:to + n, :] for _, to, n in runs(row, result_row)], axis=0
            )
            scatter = pooled - column * center[j:j + 1, :]
            cov = scatter * inverse
            if i == j:
                trace = trace + jnp.where(diag, cov, 0.0)
                square = square + cov * cov
            else:
                square = square + 2.0 * (cov * cov)
            b[at(i), at(j)] = cov
            put(cov, i, j, bh, bl)

    step = 2 * BLK

    def squared(high, low, use):
        for p in range(NB // 2):
            take, rest = slice(p * step, (p + 1) * step), slice(p * step, width)
            cross = jnp.dot(high[take, :], low[:, rest], preferred_element_type=F32)
            panel = jnp.dot(high[take, :], high[:, rest], preferred_element_type=F32) + cross
            if p < NB // 2 - 1:
                after = slice((p + 1) * step, width)
                other = jnp.dot(low[take, :], high[:, after], preferred_element_type=F32)
            for i in (2 * p, 2 * p + 1):
                for j in range(i, NB):
                    r, c = at(i - 2 * p), at(j - 2 * p)
                    if j < 2 * p + 2:
                        value = panel[r, c] + cross[c, r].T
                    else:
                        value = panel[r, c] + other[r, at(j - 2 * p - 2)]
                    use(i, j, value)

    trace = jnp.sum(trace, axis=(0, 1), keepdims=True)
    square = jnp.sum(square, axis=(0, 1), keepdims=True)
    ridge = 0.05 * trace / width + 1e-06
    norm = jnp.sqrt(square + 2.0 * ridge * trace + width * ridge * ridge)
    inv_norm = 1.0 / norm
    inv_norm2 = inv_norm * inv_norm
    scale = lax.rsqrt(norm) / 16.0

    def half_way(i, j, value):
        cov = b[at(i), at(j)]
        value = value + (2.0 * ridge) * cov
        if i == j:
            value = value + (ridge * ridge) * eye
            cov = cov + ridge * eye
        base, base2 = cov * inv_norm, value * inv_norm2
        put(base2 - 4.5 * base, i, j, sh, sl)
        rest = 6.75 * base2 - 39.0 * base
        b[at(i), at(j)] = rest + 36.0 * eye if i == j else rest

    def rooted(i, j, value):
        put((value + b[at(i), at(j)]) * scale, i, j, bh, bl)

    squared(bh, bl, half_way)
    squared(sh, sl, rooted)

    line = jnp.concatenate([center[i:i + 1, :] for i in range(NB)], axis=1)
    c_high = line.astype(BF16).astype(F32)
    c_mid = (line - c_high).astype(BF16).astype(F32)
    c_low = line - c_high - c_mid
    which = lax.broadcasted_iota(jnp.int32, (16, width), 0)
    x_ref[n_rows:n_rows + 16, :] = jnp.where(
        which == 0, c_high,
        jnp.where(which == 1, c_mid, jnp.where(which == 2, c_low, 0.0)),
    ).astype(BF16)
    load.wait()
    stores = []
    for k, (first, size) in enumerate(CHUNKS):
        cols = slice(first, first + size)
        value = jnp.dot(x_ref[...], bh[:, cols], preferred_element_type=F32) + jnp.dot(
            x_ref[...], bl[:, cols], preferred_element_type=F32
        )
        shift = jnp.sum(value[n_rows:, :], axis=0, keepdims=True)
        o_ref[:, cols] = (value[:n_rows, :] - shift).astype(BF16)
        cols = pl.ds(first, size)
        store = pltpu.make_async_copy(o_ref.at[:, cols], o_hbm.at[:, cols], store_sem.at[k])
        store.start()
        stores.append(store)
    for store in stores:
        store.wait()


def white(pooled, x):
    width = NB * BLK
    hbm = pl.BlockSpec(memory_space=pltpu.HBM)
    return pl.pallas_call(
        white_kernel,
        name="white",
        out_shape=jax.ShapeDtypeStruct(x.shape, BF16),
        in_specs=[pl.BlockSpec(memory_space=pltpu.VMEM), hbm],
        out_specs=hbm,
        scratch_shapes=[pltpu.VMEM((x.shape[0] + 16, width), BF16), pltpu.VMEM(x.shape, BF16)]
        + [pltpu.VMEM((width, width), F32)]
        + [pltpu.VMEM((width, width), BF16)] * 4
        + [pltpu.SemaphoreType.DMA, pltpu.SemaphoreType.DMA((len(CHUNKS),))],
        compiler_params=pltpu.CompilerParams(vmem_limit_bytes=48 * 2**20),
    )(pooled, x)


def on_device(embeddings, valid):
    embeddings = pltpu.with_memory_space_constraint(embeddings, pltpu.HBM)
    valid = pltpu.with_memory_space_constraint(valid[None, :], pltpu.HBM)
    return white(pool(embeddings, valid), embeddings)


def solution(mesh):
    in_specs = (P(("wide", "narrow"), None), P(("wide", "narrow")))
    return jax.shard_map(
        on_device, mesh=mesh, in_specs=in_specs, out_specs=P(("wide", "narrow"), None), check_vma=False
    )
```

```python
import functools

import jax
import jax.numpy as jnp
from jax import lax
from jax.experimental import pallas as pl
from jax.experimental.pallas import tpu as pltpu
from jax.sharding import PartitionSpec as P

MESH = pl.DeviceIdType.MESH
F32 = jnp.float32
BF16 = jnp.bfloat16

SIZE = {"z": 8, "x": 4, "y": 8, "c": 2}
BLK = 128
NB = 8
HALF_ROWS = ((0, 3, 4, 7), (1, 2, 5, 6))
A1X, A2X = 128, 128
AX = A1X + A2X
A1P, A2P = A1X // 8, A2X // 8
BY, BX = 80, 24
BS = 4 * BX
B0 = 4 * AX
C0 = B0 + 8 * BS
D0 = C0 + 8 * BS
HALF = D0 + 8
GX = AX + 8
GB = 4 * GX
GC = GB + 8 * BY
GHALF = GC + 8 * BY
N_COPIES = 120
FAR_8 = (4, 3, 5, 2, 6, 1, 7)
FAR_4 = (2, 1, 3)


def block_place(i, j):
    half = 0 if i in HALF_ROWS[0] else 1
    row = 0
    for k in HALF_ROWS[half]:
        if k == i:
            break
        row += NB - k
    return half, (row + j - i) * BLK


def coords():
    w, n = lax.axis_index("wide"), lax.axis_index("narrow")
    return {"z": w // 4, "x": w % 4, "y": n // 2, "c": n % 2}


def moved(me, axis, step):
    at = dict(me)
    at[axis] = lax.rem(me[axis] + step + SIZE[axis], SIZE[axis])
    return at


def ident(at):
    return (at["z"] * 4 + at["x"], at["y"] * 2 + at["c"])


def order(axis):
    return {"x": FAR_4, "y": FAR_8, "z": FAR_8, "c": (1,)}[axis]


def rows(start, size):
    return pl.ds(pl.multiple_of(start, 8), size)


def summed_row(row):
    return row // AX * GX + row % AX if row < B0 else row - B0 + GB


def result_row(row):
    if row < B0:
        return row
    place, row = divmod(row - B0, BY)
    return B0 + place * BS + row


def runs(row, where):
    found = []
    for k in range(0, BLK, 16):
        to = where(row + k)
        if found and found[-1][1] + found[-1][2] == to:
            found[-1][2] += 16
        else:
            found.append([k, to, 16])
    return found


def total(own, parts):
    value = own
    for k in range(parts.shape[0]):
        value = value + parts[k]
    return value


def pool_kernel(
    x_hbm, valid_hbm, out_ref,
    x_ref, valid_ref, g, got, acc,
    r1x, r1y, r1z, s1a, s1e, s1x, r2x, r2y, r2z, s2z, s2y, r3z, r3y,
    load_sem, send_sem, recv_sem,
):
    me = coords()
    core = me["c"]
    barrier = pltpu.get_barrier_semaphore()
    count = 0
    for axes in ("zy", "x", "c"):
        for step in order(axes[0]):
            for axis in axes:
                pl.semaphore_signal(
                    barrier, inc=1, device_id=ident(moved(me, axis, step)), device_id_type=MESH
                )
                count += 1
    loads = [
        pltpu.make_async_copy(x_hbm, x_ref, load_sem.at[0]),
        pltpu.make_async_copy(valid_hbm, valid_ref, load_sem.at[1]),
    ]
    for load in loads:
        load.start()
    for load in loads:
        load.wait()

    mask = valid_ref[...].astype(F32)
    mask_half = mask.astype(BF16)
    for half in range(2):
        for i in HALF_ROWS[half]:
            left = x_ref[:, i * BLK:(i + 1) * BLK].T * mask_half
            panel = jnp.dot(left, x_ref[:, i * BLK:], preferred_element_type=F32)
            for j in range(i, NB):
                _, row = block_place(i, j)
                for k, to, n in runs(row, summed_row):
                    g[half, to:to + n, :] = panel[k:k + n, (j - i) * BLK:(j - i + 1) * BLK]
    sums = jnp.dot(
        jnp.broadcast_to(mask_half, (16, mask.shape[1])), x_ref[...], preferred_element_type=F32
    )
    valid_count = jnp.broadcast_to(jnp.sum(mask, axis=1, keepdims=True), (8, BLK))
    for part in range(4):
        to = part * GX + AX
        for i in range(NB):
            g[0, to + i:to + i + 1, :] = sums[0:1, i * BLK:(i + 1) * BLK]
        g[1, to:to + 8, :] = valid_count

    pl.semaphore_wait(barrier, count)

    used = []

    def copy(src, dst, axis, step):
        at = len(used)
        made = pltpu.make_async_remote_copy(
            src_ref=src, dst_ref=dst, send_sem=send_sem.at[at], recv_sem=recv_sem.at[at],
            device_id=ident(moved(me, axis, step)), device_id_type=MESH,
        )
        used.append(made)
        made.start()
        return made

    def sent(copies):
        for made in copies:
            made.wait_send()

    def arrive(copies):
        for made in copies:
            made.wait_recv()

    def beside(axis, step):
        return moved(me, axis, step)[axis]

    cuts = [pl.ds(GB, 8 * BY), pl.ds(GC, 8 * BY)]
    cuts += [rows(GX * beside("x", s), GX) for s in FAR_4 + (0,)]
    pair = [copy(g.at[1 - core, cut], got.at[cut], "c", 1) for cut in cuts]

    def add_pair(k):
        pair[k].wait_recv()
        acc[cuts[k], :] = g[core, cuts[k], :] + got[cuts[k], :]

    add_pair(0)
    w1y = [copy(acc.at[rows(GB + BY * beside("y", s), BY)], r1y.at[s - 1], "y", s) for s in FAR_8]
    add_pair(1)
    w1z = [copy(acc.at[rows(GC + BY * beside("z", s), BY)], r1z.at[s - 1], "z", s) for s in FAR_8]
    w1x = []
    for k, s in enumerate(FAR_4):
        add_pair(k + 2)
        w1x.append(copy(acc.at[cuts[k + 2]], r1x.at[s - 1], "x", s))
    add_pair(5)

    def quarters(value, first):
        for k in range(4):
            n = min(BX, BY - BX * k)
            s1x[k, first:first + n, :] = value[BX * k:BX * k + n, :]
            if n < BX:
                s1x[k, first + n:first + BX, :] = jnp.zeros((BX - n, BLK), F32)

    arrive(w1x)
    s1a[...] = total(acc[rows(GX * me["x"], GX), :], r1x)
    w2y = [copy(s1a.at[rows(A1P * beside("y", s), A1P)], r2y.at[s - 1], "y", s) for s in FAR_8]
    for k in range(8):
        s1e[k, 0:A2P, :] = s1a[A1X + A2P * k:A1X + A2P * (k + 1), :]
        s1e[k, A2P:A2P + 8, :] = s1a[AX:GX, :]
    w2z = [copy(s1e.at[beside("z", s)], r2z.at[s - 1], "z", s) for s in FAR_8]
    arrive(w1y)
    quarters(total(acc[rows(GB + BY * me["y"], BY), :], r1y), 0)
    arrive(w1z)
    quarters(total(acc[rows(GC + BY * me["z"], BY), :], r1z), BX)
    w2x = [copy(s1x.at[beside("x", s)], r2x.at[s - 1], "x", s) for s in FAR_4]

    sent(pair)
    arrive(w2y)
    s2z[0:A1P, :] = total(s1a[rows(A1P * me["y"], A1P), :], r2y)
    arrive(w2x)
    value = total(s1x[me["x"]], r2x)
    s2z[A1P:A1P + BX, :] = value[0:BX, :]
    w3z = [copy(s2z, r3z.at[s - 1], "z", s) for s in FAR_8]
    s2y[A2P + 8:A2P + 8 + BX, :] = value[BX:2 * BX, :]
    arrive(w2z)
    s2y[0:A2P + 8, :] = total(s1e[me["z"]], r2z)
    w3y = [copy(s2y, r3y.at[s - 1], "y", s) for s in FAR_8]

    sent(w1y + w1z + w1x)
    def share(start, size, axis):
        piece = out_ref.at[core, rows(start, size)]
        return [copy(piece, piece, axis, s) for s in order(axis)]

    ax = AX * me["x"]
    a_at, e_at = ax + A1P * me["y"], ax + A1X + A2P * me["z"]
    b_at, c_at = B0 + BS * me["y"], C0 + BS * me["z"]
    arrive(w3z)
    value = total(s2z[...], r3z)
    out_ref[core, rows(b_at + BX * me["x"], BX), :] = value[A1P:A1P + BX, :]
    w4b = share(b_at + BX * me["x"], BX, "x")
    out_ref[core, rows(a_at, A1P), :] = value[0:A1P, :]
    w4a = share(a_at, A1P, "y")
    arrive(w3y)
    value = total(s2y[...], r3y)
    out_ref[core, rows(c_at + BX * me["x"], BX), :] = value[A2P + 8:A2P + 8 + BX, :]
    w4c = share(c_at + BX * me["x"], BX, "x")
    out_ref[core, rows(e_at, A2P), :] = value[0:A2P, :]
    w4e = share(e_at, A2P, "z")
    out_ref[core, D0:HALF, :] = value[A2P:A2P + 8, :]

    sent(w2x + w2y + w2z)
    arrive(w4b)
    w5b = share(b_at, BY, "y")
    arrive(w4c)
    w5c = share(c_at, BY, "z")
    arrive(w4a)
    w5a = share(ax, A1X, "x")
    arrive(w4e)
    w5e = share(ax + A1X, A2X, "x")
    w6 = share(D0, 8, "c") + share(ax, AX, "c") + share(b_at, BY, "c") + share(c_at, BY, "c")
    sent(w3z + w3y + w4b + w4c + w4a + w4e)
    for s in (1, 7, 2, 6, 3, 5, 4):
        k = FAR_8.index(s)
        w5b[k].wait_recv()
        w6 += share(B0 + BS * beside("y", -s), BY, "c")
        w5c[k].wait_recv()
        w6 += share(C0 + BS * beside("z", -s), BY, "c")
        if s in (7, 6, 5):
            k = (7, 6, 5).index(s)
            s = (1, 3, 2)[k]
            k = FAR_4.index(s)
            w5a[k].wait_recv()
            w5e[k].wait_recv()
            w6 += share(AX * beside("x", -s), AX, "c")
    sent(w5b + w5c + w5a + w5e)
    arrive(w6)
    sent(w6)


def pool(x, valid):
    part = lambda n, r: pltpu.VMEM((n, r, BLK), F32)
    flat = lambda r: pltpu.VMEM((r, BLK), F32)
    return pl.pallas_call(
        pool_kernel,
        name="pool",
        out_shape=jax.ShapeDtypeStruct((2, HALF, BLK), F32),
        in_specs=[pl.BlockSpec(memory_space=pltpu.HBM)] * 2,
        out_specs=pl.BlockSpec(memory_space=pltpu.VMEM),
        scratch_shapes=[
            pltpu.VMEM(x.shape, BF16), pltpu.VMEM(valid.shape, jnp.int32),
            part(2, GHALF), flat(GHALF), flat(GHALF),
            part(3, GX), part(7, BY), part(7, BY),
            flat(GX), part(8, A2P + 8), part(4, 2 * BX),
            part(3, 2 * BX), part(7, A1P), part(7, A2P + 8),
            flat(A1P + BX), flat(A2P + 8 + BX), part(7, A1P + BX), part(7, A2P + 8 + BX),
            pltpu.SemaphoreType.DMA((2,)),
            pltpu.SemaphoreType.DMA((N_COPIES,)), pltpu.SemaphoreType.DMA((N_COPIES,)),
        ],
        compiler_params=pltpu.CompilerParams(
            collective_id=0, has_side_effects=True, vmem_limit_bytes=40 * 2**20
        ),
    )(x, valid)


CHUNKS = ((0, 512), (512, 256), (768, 256))


def split(value):
    high = value.astype(BF16)
    return high, (value - high.astype(F32)).astype(BF16)


def white_kernel(f_ref, x_hbm, o_hbm, x_ref, o_ref, b, bh, bl, sh, sl, load_sem, store_sem):
    width = NB * BLK
    n_rows = x_hbm.shape[0]
    load = pltpu.make_async_copy(x_hbm, x_ref.at[pl.ds(0, n_rows)], load_sem)
    load.start()
    count = f_ref[1, D0:D0 + 1, :]
    sums = f_ref[0, D0:D0 + 8, :]
    center = sums / count
    diag = (
        lax.broadcasted_iota(jnp.int32, (BLK, BLK), 0)
        == lax.broadcasted_iota(jnp.int32, (BLK, BLK), 1)
    )
    eye = diag.astype(F32)

    def at(i):
        return slice(i * BLK, (i + 1) * BLK)

    def put(value, i, j, high, low):
        h, l = split(value)
        high[at(i), at(j)] = h
        low[at(i), at(j)] = l
        if i != j:
            high[at(j), at(i)] = h.T
            low[at(j), at(i)] = l.T

    trace = jnp.zeros((BLK, BLK), F32)
    on_diag = jnp.zeros((BLK, BLK), F32)
    off_diag = jnp.zeros((BLK, BLK), F32)
    for i in range(NB):
        column = jnp.broadcast_to(sums[i:i + 1, :], (BLK, BLK)).T
        for j in range(i, NB):
            half, row = block_place(i, j)
            pooled = jnp.concatenate(
                [f_ref[half, to:to + n, :] for _, to, n in runs(row, result_row)], axis=0
            )
            scatter = pooled - column * center[j:j + 1, :]
            if i == j:
                trace = trace + jnp.where(diag, scatter, 0.0)
                on_diag = on_diag + scatter * scatter
            else:
                off_diag = off_diag + scatter * scatter
            b[at(i), at(j)] = scatter
            put(scatter, i, j, bh, bl)

    step = 2 * BLK

    def squared(high, low, use):
        for p in range(NB // 2):
            take, rest = slice(p * step, (p + 1) * step), slice(p * step, width)
            cross = jnp.dot(high[take, :], low[:, rest], preferred_element_type=F32)
            panel = jnp.dot(high[take, :], high[:, rest], preferred_element_type=F32) + cross
            if p < NB // 2 - 1:
                after = slice((p + 1) * step, width)
                other = jnp.dot(low[take, :], high[:, after], preferred_element_type=F32)
            for i in (2 * p, 2 * p + 1):
                for j in range(i, NB):
                    r, c = at(i - 2 * p), at(j - 2 * p)
                    if j < 2 * p + 2:
                        value = panel[r, c] + cross[c, r].T
                    else:
                        value = panel[r, c] + other[r, at(j - 2 * p - 2)]
                    use(i, j, value)

    inverse = 1.0 / count[:, 0:1]
    trace = jnp.sum(trace, axis=(0, 1), keepdims=True) * inverse
    square = jnp.sum(on_diag + 2.0 * off_diag, axis=(0, 1), keepdims=True) * inverse * inverse
    ridge = 0.05 * trace / width + 1e-06
    norm = jnp.sqrt(square + 2.0 * ridge * trace + width * ridge * ridge)
    inv_norm = 1.0 / norm
    scale = lax.rsqrt(norm) / 16.0
    part = jnp.sqrt(scale)

    base = (0.0 * inv_norm, inverse * inv_norm, ridge * inv_norm)
    base2 = (base[1] * base[1], 2.0 * base[1] * base[2], base[2] * base[2])
    s_of = [part * (two - 4.5 * one) for two, one in zip(base2, base)]
    rest_of = [scale * (6.75 * two - 39.0 * one) for two, one in zip(base2, base)]
    rest_of[2] = rest_of[2] + 36.0 * scale

    def half_way(i, j, value):
        own = b[at(i), at(j)]
        s = s_of[0] * value + s_of[1] * own
        rest = rest_of[0] * value + rest_of[1] * own
        if i == j:
            s, rest = s + s_of[2] * eye, rest + rest_of[2] * eye
        put(s, i, j, sh, sl)
        b[at(i), at(j)] = rest

    def rooted(i, j, value):
        put(value + b[at(i), at(j)], i, j, bh, bl)

    squared(bh, bl, half_way)
    squared(sh, sl, rooted)

    line = jnp.concatenate([center[i:i + 1, :] for i in range(NB)], axis=1)
    c_high = line.astype(BF16).astype(F32)
    c_mid = (line - c_high).astype(BF16).astype(F32)
    c_low = line - c_high - c_mid
    which = lax.broadcasted_iota(jnp.int32, (16, width), 0)
    x_ref[n_rows:n_rows + 16, :] = jnp.where(
        which == 0, c_high,
        jnp.where(which == 1, c_mid, jnp.where(which == 2, c_low, 0.0)),
    ).astype(BF16)
    load.wait()
    stores = []
    for k, (first, size) in enumerate(CHUNKS):
        cols = slice(first, first + size)
        value = jnp.dot(x_ref[...], bh[:, cols], preferred_element_type=F32) + jnp.dot(
            x_ref[...], bl[:, cols], preferred_element_type=F32
        )
        shift = jnp.sum(value[n_rows:, :], axis=0, keepdims=True)
        o_ref[:, cols] = (value[:n_rows, :] - shift).astype(BF16)
        cols = pl.ds(first, size)
        store = pltpu.make_async_copy(o_ref.at[:, cols], o_hbm.at[:, cols], store_sem.at[k])
        store.start()
        stores.append(store)
    for store in stores:
        store.wait()


def white(pooled, x):
    width = NB * BLK
    hbm = pl.BlockSpec(memory_space=pltpu.HBM)
    return pl.pallas_call(
        white_kernel,
        name="white",
        out_shape=jax.ShapeDtypeStruct(x.shape, BF16),
        in_specs=[pl.BlockSpec(memory_space=pltpu.VMEM), hbm],
        out_specs=hbm,
        scratch_shapes=[pltpu.VMEM((x.shape[0] + 16, width), BF16), pltpu.VMEM(x.shape, BF16)]
        + [pltpu.VMEM((width, width), F32)]
        + [pltpu.VMEM((width, width), BF16)] * 4
        + [pltpu.SemaphoreType.DMA, pltpu.SemaphoreType.DMA((len(CHUNKS),))],
        compiler_params=pltpu.CompilerParams(vmem_limit_bytes=48 * 2**20),
    )(pooled, x)


def on_device(embeddings, valid):
    embeddings = pltpu.with_memory_space_constraint(embeddings, pltpu.HBM)
    valid = pltpu.with_memory_space_constraint(valid[None, :], pltpu.HBM)
    return white(pool(embeddings, valid), embeddings)


def solution(mesh):
    in_specs = (P(("wide", "narrow"), None), P(("wide", "narrow")))
    return jax.shard_map(
        on_device, mesh=mesh, in_specs=in_specs, out_specs=P(("wide", "narrow"), None), check_vma=False
    )
```

```python
import functools

import jax
import jax.numpy as jnp
from jax import lax
from jax.experimental import pallas as pl
from jax.experimental.pallas import tpu as pltpu
from jax.sharding import PartitionSpec as P

MESH = pl.DeviceIdType.MESH
F32 = jnp.float32
BF16 = jnp.bfloat16

SIZE = {"z": 8, "x": 4, "y": 8, "c": 2}
BLK = 128
NB = 8
HALF_ROWS = ((0, 3, 4, 7), (1, 2, 5, 6))
A1X, A2X = 128, 128
AX = A1X + A2X
A1P, A2P = A1X // 8, A2X // 8
BY, BX = 80, 24
BS = 4 * BX
B0 = 4 * AX
C0 = B0 + 8 * BS
D0 = C0 + 8 * BS
HALF = D0 + 8
GX = AX + 8
GB = 4 * GX
GC = GB + 8 * BY
GHALF = GC + 8 * BY
N_COPIES = 120
FAR_8 = (4, 3, 5, 2, 6, 1, 7)
FAR_4 = (2, 1, 3)


def block_place(i, j):
    half = 0 if i in HALF_ROWS[0] else 1
    row = 0
    for k in HALF_ROWS[half]:
        if k == i:
            break
        row += NB - k
    return half, (row + j - i) * BLK


def coords():
    w, n = lax.axis_index("wide"), lax.axis_index("narrow")
    return {"z": w // 4, "x": w % 4, "y": n // 2, "c": n % 2}


def moved(me, axis, step):
    at = dict(me)
    at[axis] = lax.rem(me[axis] + step + SIZE[axis], SIZE[axis])
    return at


def ident(at):
    return (at["z"] * 4 + at["x"], at["y"] * 2 + at["c"])


def order(axis):
    return {"x": FAR_4, "y": FAR_8, "z": FAR_8, "c": (1,)}[axis]


def rows(start, size):
    return pl.ds(pl.multiple_of(start, 8), size)


def summed_row(row):
    return row // AX * GX + row % AX if row < B0 else row - B0 + GB


def result_row(row):
    if row < B0:
        return row
    place, row = divmod(row - B0, BY)
    return B0 + place * BS + row


def runs(row, where):
    found = []
    for k in range(0, BLK, 16):
        to = where(row + k)
        if found and found[-1][1] + found[-1][2] == to:
            found[-1][2] += 16
        else:
            found.append([k, to, 16])
    return found


def total(own, parts):
    value = own
    for k in range(parts.shape[0]):
        value = value + parts[k]
    return value


def pool_kernel(
    x_hbm, valid_hbm, out_ref,
    x_ref, valid_ref, g, got, acc,
    r1x, r1y, r1z, s1a, s1e, s1x, r2x, r2y, r2z, s2z, s2y, r3z, r3y,
    load_sem, send_sem, recv_sem,
):
    me = coords()
    core = me["c"]
    barrier = pltpu.get_barrier_semaphore()
    count = 0
    for axes in ("zy", "x", "c"):
        for step in order(axes[0]):
            for axis in axes:
                pl.semaphore_signal(
                    barrier, inc=1, device_id=ident(moved(me, axis, step)), device_id_type=MESH
                )
                count += 1
    loads = [
        pltpu.make_async_copy(x_hbm, x_ref, load_sem.at[0]),
        pltpu.make_async_copy(valid_hbm, valid_ref, load_sem.at[1]),
    ]
    for load in loads:
        load.start()
    for load in loads:
        load.wait()

    mask = valid_ref[...].astype(F32)
    mask_half = mask.astype(BF16)
    for half in range(2):
        for i in HALF_ROWS[half]:
            left = x_ref[:, i * BLK:(i + 1) * BLK].T * mask_half
            panel = jnp.dot(left, x_ref[:, i * BLK:], preferred_element_type=F32)
            for j in range(i, NB):
                _, row = block_place(i, j)
                for k, to, n in runs(row, summed_row):
                    g[half, to:to + n, :] = panel[k:k + n, (j - i) * BLK:(j - i + 1) * BLK]
    sums = jnp.dot(
        jnp.broadcast_to(mask_half, (16, mask.shape[1])), x_ref[...], preferred_element_type=F32
    )
    valid_count = jnp.broadcast_to(jnp.sum(mask, axis=1, keepdims=True), (8, BLK))
    for part in range(4):
        to = part * GX + AX
        for i in range(NB):
            g[0, to + i:to + i + 1, :] = sums[0:1, i * BLK:(i + 1) * BLK]
        g[1, to:to + 8, :] = valid_count

    pl.semaphore_wait(barrier, count)

    used = []

    def copy(src, dst, axis, step):
        at = len(used)
        made = pltpu.make_async_remote_copy(
            src_ref=src, dst_ref=dst, send_sem=send_sem.at[at], recv_sem=recv_sem.at[at],
            device_id=ident(moved(me, axis, step)), device_id_type=MESH,
        )
        used.append(made)
        made.start()
        return made

    def sent(copies):
        for made in copies:
            made.wait_send()

    def arrive(copies):
        for made in copies:
            made.wait_recv()

    def beside(axis, step):
        return moved(me, axis, step)[axis]

    cuts = [pl.ds(GB, 8 * BY), rows(GX * beside("x", 2), GX), pl.ds(GC, 8 * BY)]
    cuts += [rows(GX * beside("x", s), GX) for s in (1, 3, 0)]
    pair = [copy(g.at[1 - core, cut], got.at[cut], "c", 1) for cut in cuts]

    def add_pair(k):
        pair[k].wait_recv()
        acc[cuts[k], :] = g[core, cuts[k], :] + got[cuts[k], :]

    add_pair(0)
    w1y = [copy(acc.at[rows(GB + BY * beside("y", s), BY)], r1y.at[s - 1], "y", s) for s in FAR_8]
    w1x = []
    add_pair(1)
    w1x.append(copy(acc.at[cuts[1]], r1x.at[1], "x", 2))
    add_pair(2)
    w1z = [copy(acc.at[rows(GC + BY * beside("z", s), BY)], r1z.at[s - 1], "z", s) for s in FAR_8]
    for k, s in ((3, 1), (4, 3)):
        add_pair(k)
        w1x.append(copy(acc.at[cuts[k]], r1x.at[s - 1], "x", s))
    add_pair(5)

    def quarters(value, first):
        for k in range(4):
            n = min(BX, BY - BX * k)
            s1x[k, first:first + n, :] = value[BX * k:BX * k + n, :]
            if n < BX:
                s1x[k, first + n:first + BX, :] = jnp.zeros((BX - n, BLK), F32)

    arrive(w1x)
    s1a[...] = total(acc[rows(GX * me["x"], GX), :], r1x)
    w2y = [copy(s1a.at[rows(A1P * beside("y", s), A1P)], r2y.at[s - 1], "y", s) for s in FAR_8]
    for k in range(8):
        s1e[k, 0:A2P, :] = s1a[A1X + A2P * k:A1X + A2P * (k + 1), :]
        s1e[k, A2P:A2P + 8, :] = s1a[AX:GX, :]
    w2z = [copy(s1e.at[beside("z", s)], r2z.at[s - 1], "z", s) for s in FAR_8]
    arrive(w1y)
    quarters(total(acc[rows(GB + BY * me["y"], BY), :], r1y), 0)
    arrive(w1z)
    quarters(total(acc[rows(GC + BY * me["z"], BY), :], r1z), BX)
    w2x = [copy(s1x.at[beside("x", s)], r2x.at[s - 1], "x", s) for s in FAR_4]

    sent(pair)
    arrive(w2y)
    s2z[0:A1P, :] = total(s1a[rows(A1P * me["y"], A1P), :], r2y)
    arrive(w2x)
    value = total(s1x[me["x"]], r2x)
    s2z[A1P:A1P + BX, :] = value[0:BX, :]
    w3z = [copy(s2z, r3z.at[s - 1], "z", s) for s in FAR_8]
    s2y[A2P + 8:A2P + 8 + BX, :] = value[BX:2 * BX, :]
    arrive(w2z)
    s2y[0:A2P + 8, :] = total(s1e[me["z"]], r2z)
    w3y = [copy(s2y, r3y.at[s - 1], "y", s) for s in FAR_8]

    sent(w1y + w1z + w1x)
    def share(start, size, axis):
        piece = out_ref.at[core, rows(start, size)]
        return [copy(piece, piece, axis, s) for s in order(axis)]

    ax = AX * me["x"]
    a_at, e_at = ax + A1P * me["y"], ax + A1X + A2P * me["z"]
    b_at, c_at = B0 + BS * me["y"], C0 + BS * me["z"]
    arrive(w3z)
    value = total(s2z[...], r3z)
    out_ref[core, rows(b_at + BX * me["x"], BX), :] = value[A1P:A1P + BX, :]
    w4b = share(b_at + BX * me["x"], BX, "x")
    out_ref[core, rows(a_at, A1P), :] = value[0:A1P, :]
    w4a = share(a_at, A1P, "y")
    arrive(w3y)
    value = total(s2y[...], r3y)
    out_ref[core, rows(c_at + BX * me["x"], BX), :] = value[A2P + 8:A2P + 8 + BX, :]
    w4c = share(c_at + BX * me["x"], BX, "x")
    out_ref[core, rows(e_at, A2P), :] = value[0:A2P, :]
    w4e = share(e_at, A2P, "z")
    out_ref[core, D0:HALF, :] = value[A2P:A2P + 8, :]

    sent(w2x + w2y + w2z)
    arrive(w4b)
    w5b = share(b_at, BY, "y")
    arrive(w4c)
    w5c = share(c_at, BY, "z")
    arrive(w4a)
    w5a = share(ax, A1X, "x")
    arrive(w4e)
    w5e = share(ax + A1X, A2X, "x")
    w6 = share(D0, 8, "c") + share(ax, AX, "c") + share(b_at, BY, "c") + share(c_at, BY, "c")
    sent(w3z + w3y + w4b + w4c + w4a + w4e)
    for s in (1, 7, 2, 6, 3, 5, 4):
        k = FAR_8.index(s)
        w5b[k].wait_recv()
        w6 += share(B0 + BS * beside("y", -s), BY, "c")
        w5c[k].wait_recv()
        w6 += share(C0 + BS * beside("z", -s), BY, "c")
        if s in (7, 6, 5):
            k = (7, 6, 5).index(s)
            s = (1, 3, 2)[k]
            k = FAR_4.index(s)
            w5a[k].wait_recv()
            w5e[k].wait_recv()
            w6 += share(AX * beside("x", -s), AX, "c")
    sent(w5b + w5c + w5a + w5e)
    arrive(w6)
    sent(w6)


def pool(x, valid):
    part = lambda n, r: pltpu.VMEM((n, r, BLK), F32)
    flat = lambda r: pltpu.VMEM((r, BLK), F32)
    return pl.pallas_call(
        pool_kernel,
        name="pool",
        out_shape=jax.ShapeDtypeStruct((2, HALF, BLK), F32),
        in_specs=[pl.BlockSpec(memory_space=pltpu.HBM)] * 2,
        out_specs=pl.BlockSpec(memory_space=pltpu.VMEM),
        scratch_shapes=[
            pltpu.VMEM(x.shape, BF16), pltpu.VMEM(valid.shape, jnp.int32),
            part(2, GHALF), flat(GHALF), flat(GHALF),
            part(3, GX), part(7, BY), part(7, BY),
            flat(GX), part(8, A2P + 8), part(4, 2 * BX),
            part(3, 2 * BX), part(7, A1P), part(7, A2P + 8),
            flat(A1P + BX), flat(A2P + 8 + BX), part(7, A1P + BX), part(7, A2P + 8 + BX),
            pltpu.SemaphoreType.DMA((2,)),
            pltpu.SemaphoreType.DMA((N_COPIES,)), pltpu.SemaphoreType.DMA((N_COPIES,)),
        ],
        compiler_params=pltpu.CompilerParams(
            collective_id=0, has_side_effects=True, vmem_limit_bytes=40 * 2**20
        ),
    )(x, valid)


def split(value):
    high = value.astype(BF16)
    return high, (value - high.astype(F32)).astype(BF16)


def white_kernel(f_ref, x_hbm, o_hbm, x_ref, o_ref, b, bh, bl, sh, sl, load_sem, store_sem):
    width = NB * BLK
    n_rows = x_hbm.shape[0]
    load = pltpu.make_async_copy(x_hbm, x_ref.at[pl.ds(0, n_rows)], load_sem)
    load.start()
    count = f_ref[1, D0:D0 + 1, :]
    sums = f_ref[0, D0:D0 + 8, :]
    center = sums / count
    diag = (
        lax.broadcasted_iota(jnp.int32, (BLK, BLK), 0)
        == lax.broadcasted_iota(jnp.int32, (BLK, BLK), 1)
    )
    eye = diag.astype(F32)

    def at(i):
        return slice(i * BLK, (i + 1) * BLK)

    def put(value, i, j, high, low):
        h, l = split(value)
        high[at(i), at(j)] = h
        low[at(i), at(j)] = l
        if i != j:
            high[at(j), at(i)] = h.T
            low[at(j), at(i)] = l.T

    trace = jnp.zeros((BLK, BLK), F32)
    on_diag = jnp.zeros((BLK, BLK), F32)
    off_diag = jnp.zeros((BLK, BLK), F32)
    for i in range(NB):
        column = jnp.broadcast_to(sums[i:i + 1, :], (BLK, BLK)).T
        for j in range(i, NB):
            half, row = block_place(i, j)
            pooled = jnp.concatenate(
                [f_ref[half, to:to + n, :] for _, to, n in runs(row, result_row)], axis=0
            )
            scatter = pooled - column * center[j:j + 1, :]
            if i == j:
                trace = trace + jnp.where(diag, scatter, 0.0)
                on_diag = on_diag + scatter * scatter
            else:
                off_diag = off_diag + scatter * scatter
            b[at(i), at(j)] = scatter
            put(scatter, i, j, bh, bl)

    step = 2 * BLK

    def squared(high, low, use):
        for p in range(NB // 2):
            take, rest = slice(p * step, (p + 1) * step), slice(p * step, width)
            cross = jnp.dot(high[take, :], low[:, rest], preferred_element_type=F32)
            panel = jnp.dot(high[take, :], high[:, rest], preferred_element_type=F32) + cross
            if p < NB // 2 - 1:
                after = slice((p + 1) * step, width)
                other = jnp.dot(low[take, :], high[:, after], preferred_element_type=F32)
            for i in (2 * p, 2 * p + 1):
                for j in range(i, NB):
                    r, c = at(i - 2 * p), at(j - 2 * p)
                    if j < 2 * p + 2:
                        value = panel[r, c] + cross[c, r].T
                    else:
                        value = panel[r, c] + other[r, at(j - 2 * p - 2)]
                    use(i, j, value)

    inverse = 1.0 / count[:, 0:1]
    trace = jnp.sum(trace, axis=(0, 1), keepdims=True) * inverse
    square = jnp.sum(on_diag + 2.0 * off_diag, axis=(0, 1), keepdims=True) * inverse * inverse
    ridge = 0.05 * trace / width + 1e-06
    norm = jnp.sqrt(square + 2.0 * ridge * trace + width * ridge * ridge)
    inv_norm = 1.0 / norm
    scale = lax.rsqrt(norm) / 16.0
    part = jnp.sqrt(scale)

    base = (0.0 * inv_norm, inverse * inv_norm, ridge * inv_norm)
    base2 = (base[1] * base[1], 2.0 * base[1] * base[2], base[2] * base[2])
    s_of = [part * (two - 4.5 * one) for two, one in zip(base2, base)]
    rest_of = [scale * (6.75 * two - 39.0 * one) for two, one in zip(base2, base)]
    rest_of[2] = rest_of[2] + 36.0 * scale

    def half_way(i, j, value):
        own = b[at(i), at(j)]
        s = s_of[0] * value + s_of[1] * own
        rest = rest_of[0] * value + rest_of[1] * own
        if i == j:
            s, rest = s + s_of[2] * eye, rest + rest_of[2] * eye
        put(s, i, j, sh, sl)
        b[at(i), at(j)] = rest

    def rooted(i, j, value):
        put(value + b[at(i), at(j)], i, j, bh, bl)

    squared(bh, bl, half_way)
    squared(sh, sl, rooted)

    line = jnp.concatenate([center[i:i + 1, :] for i in range(NB)], axis=1)
    c_high = line.astype(BF16).astype(F32)
    c_mid = (line - c_high).astype(BF16).astype(F32)
    c_low = line - c_high - c_mid
    which = lax.broadcasted_iota(jnp.int32, (16, width), 0)
    x_ref[n_rows:n_rows + 16, :] = jnp.where(
        which == 0, c_high,
        jnp.where(which == 1, c_mid, jnp.where(which == 2, c_low, 0.0)),
    ).astype(BF16)
    load.wait()

    def store(k):
        cols = pl.ds(pl.multiple_of(k * step, step), step)
        return pltpu.make_async_copy(o_ref.at[:, cols], o_hbm.at[:, cols], store_sem.at[k])

    @pl.loop(0, width // step)
    def _(k):
        cols = pl.ds(pl.multiple_of(k * step, step), step)
        value = jnp.dot(x_ref[...], bh[:, cols], preferred_element_type=F32) + jnp.dot(
            x_ref[...], bl[:, cols], preferred_element_type=F32
        )
        shift = jnp.sum(value[n_rows:, :], axis=0, keepdims=True)
        o_ref[:, cols] = (value[:n_rows, :] - shift).astype(BF16)
        store(k).start()

    @pl.loop(0, width // step)
    def _(k):
        store(k).wait()


def white(pooled, x):
    width = NB * BLK
    hbm = pl.BlockSpec(memory_space=pltpu.HBM)
    return pl.pallas_call(
        white_kernel,
        name="white",
        out_shape=jax.ShapeDtypeStruct(x.shape, BF16),
        in_specs=[pl.BlockSpec(memory_space=pltpu.VMEM), hbm],
        out_specs=hbm,
        scratch_shapes=[pltpu.VMEM((x.shape[0] + 16, width), BF16), pltpu.VMEM(x.shape, BF16)]
        + [pltpu.VMEM((width, width), F32)]
        + [pltpu.VMEM((width, width), BF16)] * 4
        + [pltpu.SemaphoreType.DMA, pltpu.SemaphoreType.DMA((width // (2 * BLK),))],
        compiler_params=pltpu.CompilerParams(vmem_limit_bytes=48 * 2**20),
    )(pooled, x)


def on_device(embeddings, valid):
    embeddings = pltpu.with_memory_space_constraint(embeddings, pltpu.HBM)
    valid = pltpu.with_memory_space_constraint(valid[None, :], pltpu.HBM)
    return white(pool(embeddings, valid), embeddings)


def solution(mesh):
    in_specs = (P(("wide", "narrow"), None), P(("wide", "narrow")))
    return jax.shard_map(
        on_device, mesh=mesh, in_specs=in_specs, out_specs=P(("wide", "narrow"), None), check_vma=False
    )
```

```python
import functools

import jax
import jax.numpy as jnp
from jax import lax
from jax.experimental import pallas as pl
from jax.experimental.pallas import tpu as pltpu
from jax.sharding import PartitionSpec as P

MESH = pl.DeviceIdType.MESH
F32 = jnp.float32
BF16 = jnp.bfloat16

SIZE = {"z": 8, "x": 4, "y": 8, "c": 2}
BLK = 128
NB = 8
HALF_ROWS = ((0, 3, 4, 7), (1, 2, 5, 6))
A1X, A2X = 128, 128
AX = A1X + A2X
A1P, A2P = A1X // 8, A2X // 8
BY, BX = 80, 24
BS = 4 * BX
B0 = 4 * AX
C0 = B0 + 8 * BS
D0 = C0 + 8 * BS
HALF = D0 + 8
GX = AX + 8
GB = 4 * GX
GC = GB + 8 * BY
GHALF = GC + 8 * BY
N_COPIES = 120
FAR_8 = (4, 3, 5, 2, 6, 1, 7)
FAR_4 = (2, 1, 3)


def block_place(i, j):
    half = 0 if i in HALF_ROWS[0] else 1
    row = 0
    for k in HALF_ROWS[half]:
        if k == i:
            break
        row += NB - k
    return half, (row + j - i) * BLK


def coords():
    w, n = lax.axis_index("wide"), lax.axis_index("narrow")
    return {"z": w // 4, "x": w % 4, "y": n // 2, "c": n % 2}


def moved(me, axis, step):
    at = dict(me)
    at[axis] = lax.rem(me[axis] + step + SIZE[axis], SIZE[axis])
    return at


def ident(at):
    return (at["z"] * 4 + at["x"], at["y"] * 2 + at["c"])


def order(axis):
    return {"x": FAR_4, "y": FAR_8, "z": FAR_8, "c": (1,)}[axis]


def rows(start, size):
    return pl.ds(pl.multiple_of(start, 8), size)


def summed_row(row):
    return row // AX * GX + row % AX if row < B0 else row - B0 + GB


def result_row(row):
    if row < B0:
        return row
    place, row = divmod(row - B0, BY)
    return B0 + place * BS + row


def runs(row, where):
    found = []
    for k in range(0, BLK, 16):
        to = where(row + k)
        if found and found[-1][1] + found[-1][2] == to:
            found[-1][2] += 16
        else:
            found.append([k, to, 16])
    return found


def total(own, parts):
    value = own
    for k in range(parts.shape[0]):
        value = value + parts[k]
    return value


def pool_kernel(
    x_hbm, valid_hbm, out_ref,
    x_ref, valid_ref, g, got, acc,
    r1x, r1y, r1z, s1a, s1e, s1x, r2x, r2y, r2z, s2z, s2y, r3z, r3y,
    load_sem, send_sem, recv_sem,
):
    me = coords()
    core = me["c"]
    barrier = pltpu.get_barrier_semaphore()
    count = 0
    for axes in ("zy", "x", "c"):
        for step in order(axes[0]):
            for axis in axes:
                pl.semaphore_signal(
                    barrier, inc=1, device_id=ident(moved(me, axis, step)), device_id_type=MESH
                )
                count += 1
    loads = [
        pltpu.make_async_copy(x_hbm, x_ref, load_sem.at[0]),
        pltpu.make_async_copy(valid_hbm, valid_ref, load_sem.at[1]),
    ]
    for load in loads:
        load.start()
    for load in loads:
        load.wait()

    mask = valid_ref[...].astype(F32)
    mask_half = mask.astype(BF16)
    for half in range(2):
        for i in HALF_ROWS[half]:
            left = x_ref[:, i * BLK:(i + 1) * BLK].T * mask_half
            panel = jnp.dot(left, x_ref[:, i * BLK:], preferred_element_type=F32)
            for j in range(i, NB):
                _, row = block_place(i, j)
                for k, to, n in runs(row, summed_row):
                    g[half, to:to + n, :] = panel[k:k + n, (j - i) * BLK:(j - i + 1) * BLK]
    sums = jnp.dot(
        jnp.broadcast_to(mask_half, (16, mask.shape[1])), x_ref[...], preferred_element_type=F32
    )
    valid_count = jnp.broadcast_to(jnp.sum(mask, axis=1, keepdims=True), (8, BLK))
    for part in range(4):
        to = part * GX + AX
        for i in range(NB):
            g[0, to + i:to + i + 1, :] = sums[0:1, i * BLK:(i + 1) * BLK]
        g[1, to:to + 8, :] = valid_count

    pl.semaphore_wait(barrier, count)

    used = []

    def copy(src, dst, axis, step):
        at = len(used)
        made = pltpu.make_async_remote_copy(
            src_ref=src, dst_ref=dst, send_sem=send_sem.at[at], recv_sem=recv_sem.at[at],
            device_id=ident(moved(me, axis, step)), device_id_type=MESH,
        )
        used.append(made)
        made.start()
        return made

    def sent(copies):
        for made in copies:
            made.wait_send()

    def arrive(copies):
        for made in copies:
            made.wait_recv()

    def beside(axis, step):
        return moved(me, axis, step)[axis]

    cuts = [pl.ds(GB, 8 * BY), rows(GX * beside("x", 2), GX), pl.ds(GC, 8 * BY)]
    cuts += [rows(GX * beside("x", s), GX) for s in (1, 3, 0)]
    pair = [copy(g.at[1 - core, cut], got.at[cut], "c", 1) for cut in cuts]

    def add_pair(k):
        pair[k].wait_recv()
        acc[cuts[k], :] = g[core, cuts[k], :] + got[cuts[k], :]

    add_pair(0)
    w1y = [copy(acc.at[rows(GB + BY * beside("y", s), BY)], r1y.at[s - 1], "y", s) for s in FAR_8]
    w1x = []
    add_pair(1)
    w1x.append(copy(acc.at[cuts[1]], r1x.at[1], "x", 2))
    add_pair(2)
    w1z = [copy(acc.at[rows(GC + BY * beside("z", s), BY)], r1z.at[s - 1], "z", s) for s in FAR_8]
    for k, s in ((3, 1), (4, 3)):
        add_pair(k)
        w1x.append(copy(acc.at[cuts[k]], r1x.at[s - 1], "x", s))
    add_pair(5)

    def quarters(value, first):
        for k in range(4):
            n = min(BX, BY - BX * k)
            s1x[k, first:first + n, :] = value[BX * k:BX * k + n, :]
            if n < BX:
                s1x[k, first + n:first + BX, :] = jnp.zeros((BX - n, BLK), F32)

    arrive(w1x)
    s1a[...] = total(acc[rows(GX * me["x"], GX), :], r1x)
    w2y = [copy(s1a.at[rows(A1P * beside("y", s), A1P)], r2y.at[s - 1], "y", s) for s in FAR_8]
    for k in range(8):
        s1e[k, 0:A2P, :] = s1a[A1X + A2P * k:A1X + A2P * (k + 1), :]
        s1e[k, A2P:A2P + 8, :] = s1a[AX:GX, :]
    w2z = [copy(s1e.at[beside("z", s)], r2z.at[s - 1], "z", s) for s in FAR_8]
    arrive(w1y)
    quarters(total(acc[rows(GB + BY * me["y"], BY), :], r1y), 0)
    arrive(w1z)
    quarters(total(acc[rows(GC + BY * me["z"], BY), :], r1z), BX)
    w2x = [copy(s1x.at[beside("x", s)], r2x.at[s - 1], "x", s) for s in FAR_4]

    sent(pair)
    arrive(w2y)
    s2z[0:A1P, :] = total(s1a[rows(A1P * me["y"], A1P), :], r2y)
    arrive(w2x)
    value = total(s1x[me["x"]], r2x)
    s2z[A1P:A1P + BX, :] = value[0:BX, :]
    w3z = [copy(s2z, r3z.at[s - 1], "z", s) for s in FAR_8]
    s2y[A2P + 8:A2P + 8 + BX, :] = value[BX:2 * BX, :]
    arrive(w2z)
    s2y[0:A2P + 8, :] = total(s1e[me["z"]], r2z)
    w3y = [copy(s2y, r3y.at[s - 1], "y", s) for s in FAR_8]

    sent(w1y + w1z + w1x)
    def share(start, size, axis):
        piece = out_ref.at[core, rows(start, size)]
        return [copy(piece, piece, axis, s) for s in order(axis)]

    ax = AX * me["x"]
    a_at, e_at = ax + A1P * me["y"], ax + A1X + A2P * me["z"]
    b_at, c_at = B0 + BS * me["y"], C0 + BS * me["z"]
    arrive(w3z)
    value = total(s2z[...], r3z)
    out_ref[core, rows(b_at + BX * me["x"], BX), :] = value[A1P:A1P + BX, :]
    w4b = share(b_at + BX * me["x"], BX, "x")
    out_ref[core, rows(a_at, A1P), :] = value[0:A1P, :]
    w4a = share(a_at, A1P, "y")
    arrive(w3y)
    value = total(s2y[...], r3y)
    out_ref[core, rows(c_at + BX * me["x"], BX), :] = value[A2P + 8:A2P + 8 + BX, :]
    w4c = share(c_at + BX * me["x"], BX, "x")
    out_ref[core, rows(e_at, A2P), :] = value[0:A2P, :]
    w4e = share(e_at, A2P, "z")
    out_ref[core, D0:HALF, :] = value[A2P:A2P + 8, :]

    sent(w2x + w2y + w2z)
    arrive(w4b)
    w5b = share(b_at, BY, "y")
    arrive(w4c)
    w5c = share(c_at, BY, "z")
    arrive(w4a)
    w5a = share(ax, A1X, "x")
    arrive(w4e)
    w5e = share(ax + A1X, A2X, "x")
    w6 = share(D0, 8, "c") + share(ax, AX, "c") + share(b_at, BY, "c") + share(c_at, BY, "c")
    sent(w3z + w3y + w4b + w4c + w4a + w4e)
    for s in (1, 7, 2, 6, 3, 5, 4):
        k = FAR_8.index(s)
        w5b[k].wait_recv()
        w6 += share(B0 + BS * beside("y", -s), BY, "c")
        w5c[k].wait_recv()
        w6 += share(C0 + BS * beside("z", -s), BY, "c")
        if s in (7, 6, 5):
            k = (7, 6, 5).index(s)
            s = (1, 3, 2)[k]
            k = FAR_4.index(s)
            w5a[k].wait_recv()
            w5e[k].wait_recv()
            w6 += share(AX * beside("x", -s), AX, "c")
    sent(w5b + w5c + w5a + w5e)
    arrive(w6)
    sent(w6)


def pool(x, valid):
    part = lambda n, r: pltpu.VMEM((n, r, BLK), F32)
    flat = lambda r: pltpu.VMEM((r, BLK), F32)
    return pl.pallas_call(
        pool_kernel,
        name="pool",
        out_shape=jax.ShapeDtypeStruct((2, HALF, BLK), F32),
        in_specs=[pl.BlockSpec(memory_space=pltpu.HBM)] * 2,
        out_specs=pl.BlockSpec(memory_space=pltpu.VMEM),
        scratch_shapes=[
            pltpu.VMEM(x.shape, BF16), pltpu.VMEM(valid.shape, jnp.int32),
            part(2, GHALF), flat(GHALF), flat(GHALF),
            part(3, GX), part(7, BY), part(7, BY),
            flat(GX), part(8, A2P + 8), part(4, 2 * BX),
            part(3, 2 * BX), part(7, A1P), part(7, A2P + 8),
            flat(A1P + BX), flat(A2P + 8 + BX), part(7, A1P + BX), part(7, A2P + 8 + BX),
            pltpu.SemaphoreType.DMA((2,)),
            pltpu.SemaphoreType.DMA((N_COPIES,)), pltpu.SemaphoreType.DMA((N_COPIES,)),
        ],
        compiler_params=pltpu.CompilerParams(
            collective_id=0, has_side_effects=True, vmem_limit_bytes=40 * 2**20
        ),
    )(x, valid)


CHUNKS = ((0, 512), (512, 256), (768, 256))


def split(value):
    high = value.astype(BF16)
    return high, (value - high.astype(F32)).astype(BF16)


def white_kernel(f_ref, x_hbm, o_hbm, x_ref, o_ref, b, bh, bl, sh, sl, load_sem, store_sem):
    width = NB * BLK
    n_rows = x_hbm.shape[0]
    load = pltpu.make_async_copy(x_hbm, x_ref.at[pl.ds(0, n_rows)], load_sem)
    load.start()
    count = f_ref[1, D0:D0 + 1, :]
    sums = f_ref[0, D0:D0 + 8, :]
    center = sums / count
    diag = (
        lax.broadcasted_iota(jnp.int32, (BLK, BLK), 0)
        == lax.broadcasted_iota(jnp.int32, (BLK, BLK), 1)
    )
    eye = diag.astype(F32)

    def at(i):
        return slice(i * BLK, (i + 1) * BLK)

    def put(value, i, j, high, low):
        h, l = split(value)
        high[at(i), at(j)] = h
        low[at(i), at(j)] = l
        if i != j:
            high[at(j), at(i)] = h.T
            low[at(j), at(i)] = l.T

    trace = jnp.zeros((BLK, BLK), F32)
    on_diag = jnp.zeros((BLK, BLK), F32)
    off_diag = jnp.zeros((BLK, BLK), F32)
    for i in range(NB):
        column = jnp.broadcast_to(sums[i:i + 1, :], (BLK, BLK)).T
        for j in range(i, NB):
            half, row = block_place(i, j)
            pooled = jnp.concatenate(
                [f_ref[half, to:to + n, :] for _, to, n in runs(row, result_row)], axis=0
            )
            scatter = pooled - column * center[j:j + 1, :]
            if i == j:
                trace = trace + jnp.where(diag, scatter, 0.0)
                on_diag = on_diag + scatter * scatter
            else:
                off_diag = off_diag + scatter * scatter
            b[at(i), at(j)] = scatter
            put(scatter, i, j, bh, bl)

    step = 2 * BLK

    def squared(high, low, use):
        for p in range(NB // 2):
            take, rest = slice(p * step, (p + 1) * step), slice(p * step, width)
            cross = jnp.dot(high[take, :], low[:, rest], preferred_element_type=F32)
            panel = jnp.dot(high[take, :], high[:, rest], preferred_element_type=F32) + cross
            if p < NB // 2 - 1:
                after = slice((p + 1) * step, width)
                other = jnp.dot(low[take, :], high[:, after], preferred_element_type=F32)
            for i in (2 * p, 2 * p + 1):
                for j in range(i, NB):
                    r, c = at(i - 2 * p), at(j - 2 * p)
                    if j < 2 * p + 2:
                        value = panel[r, c] + cross[c, r].T
                    else:
                        value = panel[r, c] + other[r, at(j - 2 * p - 2)]
                    use(i, j, value)

    inverse = 1.0 / count[:, 0:1]
    trace = jnp.sum(trace, axis=(0, 1), keepdims=True) * inverse
    square = jnp.sum(on_diag + 2.0 * off_diag, axis=(0, 1), keepdims=True) * inverse * inverse
    ridge = 0.05 * trace / width + 1e-06
    norm = jnp.sqrt(square + 2.0 * ridge * trace + width * ridge * ridge)
    inv_norm = 1.0 / norm
    scale = lax.rsqrt(norm) / 16.0
    part = jnp.sqrt(scale)

    base = (0.0 * inv_norm, inverse * inv_norm, ridge * inv_norm)
    base2 = (base[1] * base[1], 2.0 * base[1] * base[2], base[2] * base[2])
    s_of = [part * (two - 4.5 * one) for two, one in zip(base2, base)]
    rest_of = [scale * (6.75 * two - 39.0 * one) for two, one in zip(base2, base)]
    rest_of[2] = rest_of[2] + 36.0 * scale

    def half_way(i, j, value):
        own = b[at(i), at(j)]
        s = s_of[0] * value + s_of[1] * own
        rest = rest_of[0] * value + rest_of[1] * own
        if i == j:
            s, rest = s + s_of[2] * eye, rest + rest_of[2] * eye
        put(s, i, j, sh, sl)
        b[at(i), at(j)] = rest

    def rooted(i, j, value):
        put(value + b[at(i), at(j)], i, j, bh, bl)

    squared(bh, bl, half_way)
    squared(sh, sl, rooted)

    line = jnp.concatenate([center[i:i + 1, :] for i in range(NB)], axis=1)
    c_high = line.astype(BF16).astype(F32)
    c_mid = (line - c_high).astype(BF16).astype(F32)
    c_low = line - c_high - c_mid
    which = lax.broadcasted_iota(jnp.int32, (16, width), 0)
    x_ref[n_rows:n_rows + 16, :] = jnp.where(
        which == 0, c_high,
        jnp.where(which == 1, c_mid, jnp.where(which == 2, c_low, 0.0)),
    ).astype(BF16)
    load.wait()
    stores = []
    for k, (first, size) in enumerate(CHUNKS):
        cols = slice(first, first + size)
        value = jnp.dot(x_ref[...], bh[:, cols], preferred_element_type=F32) + jnp.dot(
            x_ref[...], bl[:, cols], preferred_element_type=F32
        )
        shift = jnp.sum(value[n_rows:, :], axis=0, keepdims=True)
        o_ref[:, cols] = (value[:n_rows, :] - shift).astype(BF16)
        cols = pl.ds(first, size)
        store = pltpu.make_async_copy(o_ref.at[:, cols], o_hbm.at[:, cols], store_sem.at[k])
        store.start()
        stores.append(store)
    for store in stores:
        store.wait()


def white(pooled, x):
    width = NB * BLK
    hbm = pl.BlockSpec(memory_space=pltpu.HBM)
    return pl.pallas_call(
        white_kernel,
        name="white",
        out_shape=jax.ShapeDtypeStruct(x.shape, BF16),
        in_specs=[pl.BlockSpec(memory_space=pltpu.VMEM), hbm],
        out_specs=hbm,
        scratch_shapes=[pltpu.VMEM((x.shape[0] + 16, width), BF16), pltpu.VMEM(x.shape, BF16)]
        + [pltpu.VMEM((width, width), F32)]
        + [pltpu.VMEM((width, width), BF16)] * 4
        + [pltpu.SemaphoreType.DMA, pltpu.SemaphoreType.DMA((len(CHUNKS),))],
        compiler_params=pltpu.CompilerParams(vmem_limit_bytes=48 * 2**20),
    )(pooled, x)


def on_device(embeddings, valid):
    embeddings = pltpu.with_memory_space_constraint(embeddings, pltpu.HBM)
    valid = pltpu.with_memory_space_constraint(valid[None, :], pltpu.HBM)
    return white(pool(embeddings, valid), embeddings)


def solution(mesh):
    in_specs = (P(("wide", "narrow"), None), P(("wide", "narrow")))
    return jax.shard_map(
        on_device, mesh=mesh, in_specs=in_specs, out_specs=P(("wide", "narrow"), None), check_vma=False
    )
```
